128 devices in a mesh: dp: 4 (over x), seq: 2 (over y_hi), tensor: 16 (over z, y_lo, core).
Axes of the slice: x: 4, y: 4 (y_hi: 2, y_lo: 2; y = y_hi * 2 + y_lo), z: 4, core: 2. Of those that a mesh axis runs over, the one named last changes fastest.
Arguments:
- captured: bfloat16 [3, 4, 256, 8192], P(None, 'dp', 'seq', 'tensor'), may hold values from -6 to 6
- target_logits: bfloat16 [4, 256, 16384], P('dp', 'seq', 'tensor'), may hold values from -400 to 400
- unite_weight: bfloat16 [3, 8192, 8192], P(None, 'tensor', ('dp', 'seq')), may hold values from -0.0390625 to 0.0390625
- norm_gain: float32 [8192], replicated, may hold values from 0.1 to 1.9
- head_weight: bfloat16 [16384, 8192], P('tensor'), may hold values from -32 to 32
- lengths: int32 [4], P('dp'), may hold values from 1 to 256, 640 in all
- loss_mask: int32 [4, 256], P('dp', 'seq'), may hold values 0 or 1
Outputs:
- seq_kl: float32 [4], P('dp')
- unite_grad: float32 [3, 8192, 8192], P(None, 'tensor', ('dp', 'seq'))
The draws below stay inside these ranges and needn't reach their ends.
Inputs may be any that keep to these rules, and one draw needn't show every extreme that they name: `lengths`: some sequence has all 256 positions valid.
All inputs are finite; a program needn't handle non-finite values. No bound on the sum of `lengths` or of `loss_mask` on one device may be relied on, other than what follows from the above.
Results may differ from the reference program's by a relative error of at most 0.02.
Values may be sent and summed in bfloat16 or wider, within the bound.
No kernel may reach another device: no remote copies, remote signals or barrier semaphores. Data moves between devices by JAX's collectives and lax.ppermute only.
A program may use at most 128 MiB of HBM per device.

```python
import math
import jax
import jax.numpy as jnp
import numpy as np
from jax import lax

D = 8192
VD = 16384
LEN = 256
SEQS = 4


def draw_target_logits(key, part):
    key = jax.random.fold_in(key, 7)
    noise_key = jax.random.fold_in(key, 0)
    values = 3.0 * jax.random.normal(noise_key, (SEQS, LEN, VD), jnp.float32)
    return values.astype(jnp.bfloat16)


def draw_head_weight(key, part):
    key = jax.random.fold_in(key, 13)
    base_key = jax.random.fold_in(key, 0)
    base = jax.random.normal(base_key, (VD, D), jnp.float32) * (1.5 / math.sqrt(D))
    return base.astype(jnp.bfloat16)


def plant(entries, rng, low, high):
    place = [jax.random.randint(jax.random.fold_in(rng, axis), (), 0, length) for axis, length in enumerate(entries.shape)]
    main_axis = entries.shape.index(max(entries.shape))
    beside = place[:main_axis] + [(place[main_axis] + 1) % entries.shape[main_axis]] + place[main_axis + 1:]
    return entries.at[tuple(place)].set(low).at[tuple(beside)].set(high)


def block_scale(own_key, shape, cuts, low, top_value):
    loudness = 1.0
    for axis_at, parts in cuts:
        steps = jax.random.uniform(jax.random.fold_in(jax.random.fold_in(own_key, 6), axis_at), (parts,), jnp.float32, low / len(cuts), top_value / len(cuts))
        loudness = loudness * jnp.repeat(jnp.exp(steps), shape[axis_at] // parts).reshape((-1,) + (1,) * (len(shape) - 1 - axis_at))
    return loudness


def profile(count, total, bound, lean):
    weights = [(1 << 20) // math.isqrt(standing ** lean) + 1 for standing in range(2, count + 1)]
    surplus, counts = total - bound - (count - 1), [1] * (count - 1)
    while surplus > 0:
        movable = [i for i in range(count - 1) if counts[i] < bound]
        mass, budget = sum([weights[i] for i in movable]), surplus
        for i in movable:
            addition = min(bound - counts[i], max(1, budget * weights[i] // mass), surplus)
            counts[i] = counts[i] + addition
            surplus = surplus - addition
    return np.array([bound] + counts)


def uneven(rng, count, total, bound, slope):
    if count == 2:
        one = jax.random.randint(rng, (), max(1, total - bound), min(bound, total - 1) + 1)
        return jnp.stack([one, total - one])
    sizes = jnp.asarray(profile(count, total, bound, slope), jnp.int32)
    twos = (count - 1) // 2
    source_of, taker = sizes[1:1 + 2 * twos:2], sizes[2:2 + 2 * twos:2]
    margin = jnp.minimum(source_of - 1, bound - taker)
    passed = jax.random.randint(jax.random.fold_in(rng, 1), (twos,), 0, 1 << 20) % (margin + 1)
    sizes = sizes.at[1:1 + 2 * twos:2].set(source_of - passed).at[2:2 + 2 * twos:2].set(taker + passed)
    return sizes[jax.random.permutation(jax.random.fold_in(rng, 2), count)]


def normal_values(key, dims, width, limit, cuts=(), held_as=jnp.bfloat16):
    values = jax.random.normal(key, dims, jnp.float32) * width
    if len(cuts) > 0:
        values = block_scale(key, dims, cuts, -0.22, 0.18) * values
    return jnp.clip(values, min=-limit, max=limit).astype(held_as)


def setup_inputs(seed: int = 0) -> dict:
    arg_keys = jax.random.split(jax.random.key(seed), 8)
    captured = normal_values(arg_keys[0], (3, SEQS, LEN, D), 1.0, 6.0, ((1, 4), (2, 2), (3, 16)))
    target_logits = draw_target_logits(jax.random.fold_in(arg_keys[7], 71), 0)
    unite_weight = normal_values(arg_keys[2], (3, D, D), (3 * D) ** -0.5, 0.0390625, ((1, 16), (2, 8)))
    norm_gain = jnp.clip(1.0 + 0.18 * jax.random.normal(arg_keys[3], (D,), jnp.float32), 0.1, 1.9)
    head_weight = draw_head_weight(jax.random.fold_in(arg_keys[7], 71), 0)
    lengths = uneven(arg_keys[5], SEQS, SEQS * LEN * 5 // 8, LEN, 1).astype(jnp.int32)
    loss_mask = plant((jax.random.randint(arg_keys[6], (SEQS, LEN), 0, 4) < 3).astype(jnp.int32), jax.random.fold_in(arg_keys[6], 1), 0, 1)
    return {"captured": captured, "target_logits": target_logits, "unite_weight": unite_weight, "norm_gain": norm_gain, "head_weight": head_weight, "lengths": lengths, "loss_mask": loss_mask}


NORM_EPS = 1e-05

def reference(captured, target_logits, unite_weight, norm_gain, head_weight, lengths, loss_mask):
    token_total = captured.shape[1] * captured.shape[2]
    seq_length = captured.shape[2]
    model_width = captured.shape[3]
    streams = captured.reshape(3, token_total, model_width)
    united_sum = jnp.dot(streams[0], unite_weight[0], preferred_element_type=jnp.float32)
    united_sum = united_sum + jnp.dot(streams[1], unite_weight[1], preferred_element_type=jnp.float32)
    united_sum = united_sum + jnp.dot(streams[2], unite_weight[2], preferred_element_type=jnp.float32)
    united_rows = united_sum.astype(jnp.bfloat16)
    values = united_rows.astype(jnp.float32)
    row_scale = lax.rsqrt(lax.optimization_barrier(jnp.mean(values * values, axis=-1)) + NORM_EPS)
    normed = (values * row_scale[:, None] * norm_gain[None, :]).astype(jnp.bfloat16)
    draft_logits = jnp.dot(normed, head_weight.T, preferred_element_type=jnp.float32)
    target = target_logits.reshape(token_total, -1).astype(jnp.float32)
    log_target = jax.nn.log_softmax(target, axis=-1)
    log_draft = jax.nn.log_softmax(draft_logits, axis=-1)
    target_prob = jnp.exp(log_target)
    draft_prob = jnp.exp(log_draft)
    kl_rows = lax.optimization_barrier(jnp.sum(target_prob * (log_target - log_draft), axis=-1))
    positions = lax.broadcasted_iota(jnp.int32, loss_mask.shape, 1)
    valid_flags = ((positions < lengths[:, None]) & (loss_mask == 1)).astype(jnp.float32)
    count_seq = lax.optimization_barrier(jnp.sum(valid_flags, axis=1))
    kl_seq = lax.optimization_barrier(jnp.sum(valid_flags * kl_rows.reshape(valid_flags.shape), axis=1))
    seq_kl = kl_seq / jnp.maximum(count_seq, 1.0)
    factor = seq_length / jnp.maximum(jnp.sum(count_seq), 1.0)
    grad_logits = (valid_flags.reshape(token_total)[:, None] * (draft_prob - target_prob)).astype(jnp.bfloat16)
    grad_normed = jnp.dot(grad_logits, head_weight, preferred_element_type=jnp.float32)
    scaled = grad_normed * norm_gain[None, :]
    row_inner = lax.optimization_barrier(jnp.sum(values * scaled, axis=-1))
    grad_united = (row_scale[:, None] * scaled - (row_scale * row_scale * row_scale * row_inner / model_width)[:, None] * values).astype(jnp.bfloat16)
    pieces = []
    for stream_index in range(3):
        block = jnp.dot(streams[stream_index].T, grad_united, preferred_element_type=jnp.float32)
        pieces.append(block * factor)
    unite_grad = jnp.stack(pieces)
    return (seq_kl, unite_grad)
```

```python
import jax
import jax.numpy as jnp
from jax import lax
from jax.sharding import Mesh, PartitionSpec as P

NORM_EPS = 1e-05
GROUP = ("x", "yh")
RING = ("z", "yl")
ALL = ("x", "yh", "z", "yl", "c")


def spread(value, axes, count):
    return lax.all_to_all(
        jnp.broadcast_to(value[None], (count,) + value.shape), axes, 0, 0, tiled=True
    )


def swap_core(value):
    return lax.ppermute(value, "c", [(0, 1), (1, 0)])


def gather_tensor(piece):
    ring = spread(piece, RING, 8)
    other = swap_core(ring)
    first = lax.axis_index("c") == 0
    return jnp.stack([jnp.where(first, ring, other), jnp.where(first, other, ring)], 1)


def local(captured, target_logits, unite_weight, norm_gain, head_weight, lengths, loss_mask):
    f32, bf16 = jnp.float32, jnp.bfloat16
    half_len = captured.shape[2]
    width = norm_gain.shape[0]
    vocab = head_weight.shape[0]
    t_index = lax.axis_index(("z", "yl", "c"))
    streams = spread(captured.reshape(3, half_len, 512), GROUP, 8)

    positions = lax.axis_index("yh") * half_len + lax.iota(jnp.int32, half_len)
    valid = ((positions < lengths[0]) & (loss_mask[0] == 1)).astype(f32)
    count_part = jnp.sum(valid)
    count_all = spread(jnp.full((8, 128), count_part, f32), GROUP, 8)[:, 0, 0]
    factor = (2 * half_len) / jnp.maximum(jnp.sum(count_all), 1.0)
    count_seq = jnp.sum(
        lax.dynamic_slice_in_dim(count_all, lax.axis_index("x") * 2, 2)
    )

    partial = jnp.einsum("gsrk,skn->grn", streams, unite_weight, preferred_element_type=f32)
    pieces = lax.all_to_all(
        partial.astype(bf16).reshape(128, 8, 1024), ALL, 0, 0, tiled=True
    )
    united = jnp.sum(pieces.reshape(8, 16, 8, 1024).astype(f32), axis=1).astype(bf16)
    rows = gather_tensor(united)
    united_rows = rows.reshape(16, 8, 8, 1024).transpose(0, 2, 1, 3).reshape(128, width)

    values = united_rows.astype(f32)
    row_scale = lax.rsqrt(jnp.sum(values * values, axis=1) / width + NORM_EPS)
    normed = (values * row_scale[:, None] * norm_gain[None, :]).astype(bf16)
    logits = lax.dot_general(
        normed, head_weight, (((1,), (1,)), ((), ())), preferred_element_type=f32
    )
    target = target_logits.reshape(half_len, vocab).astype(f32)
    top_t = jnp.max(target, axis=1)
    pow_t = jnp.exp(target - top_t[:, None])
    top_d = jnp.max(logits, axis=1)
    pow_d = jnp.exp(logits - top_d[:, None])
    stats = jnp.stack(
        [
            top_t,
            jnp.sum(pow_t, axis=1),
            jnp.sum(pow_t * target, axis=1),
            jnp.sum(pow_t * logits, axis=1),
            top_d,
            jnp.sum(pow_d, axis=1),
            jnp.sum(pow_d * logits, axis=1),
            jnp.zeros_like(top_d),
        ]
    )
    every = spread(stats, ("z", "yl", "c"), 16)
    max_t = jnp.max(every[:, 0], axis=0)
    scale_t = jnp.exp(every[:, 0] - max_t)
    sum_t = jnp.sum(every[:, 1] * scale_t, axis=0)
    mean_tt = jnp.sum(every[:, 2] * scale_t, axis=0) / sum_t
    mean_tl = jnp.sum(every[:, 3] * scale_t, axis=0) / sum_t
    max_d = jnp.max(every[:, 4], axis=0)
    scale_d = jnp.exp(every[:, 4] - max_d)
    sum_d = jnp.sum(every[:, 5] * scale_d, axis=0)
    mean_dl = jnp.sum(every[:, 6] * scale_d, axis=0) / sum_d
    log_t = max_t + jnp.log(sum_t)
    log_d = max_d + jnp.log(sum_d)
    kl = mean_tt - mean_tl - log_t + log_d
    inner = valid * (mean_dl - mean_tl) / row_scale

    grad_logits = (
        valid[:, None] * (jnp.exp(logits - log_d[:, None]) - jnp.exp(target - log_t[:, None]))
    ).astype(bf16)
    grad_normed = lax.dot_general(
        grad_logits, head_weight, (((1,), (0,)), ((), ())), preferred_element_type=f32
    )
    mine = (lax.iota(jnp.int32, half_len) // 8) == t_index
    cubic = jnp.where(mine, row_scale * row_scale * row_scale * inner / width, 0.0)
    grad_part = (
        grad_normed * row_scale[:, None] * norm_gain[None, :] - cubic[:, None] * values
    ).astype(bf16)
    grad_pieces = lax.all_to_all(
        grad_part.reshape(128, 8, 1024).transpose(1, 0, 2).reshape(128, 8, 1024),
        ALL, 0, 0, tiled=True,
    )
    grad_sum = jnp.sum(grad_pieces.reshape(8, 16, 8, 1024).astype(f32), axis=1).astype(bf16)
    grad_all = gather_tensor(grad_sum).reshape(16, 8, 8, 1024).transpose(1, 0, 2, 3)
    grad_all = grad_all.reshape(8, 128, 1024)
    weight_grad = jnp.einsum("gsrk,grn->skn", streams, grad_all, preferred_element_type=f32)
    unite_grad = weight_grad * factor

    kl_part = jnp.sum(kl * valid)
    kl_all = spread(jnp.full((8, 128), kl_part, f32), ("yh",), 2)[:, 0, 0]
    seq_kl = (jnp.sum(kl_all) / jnp.maximum(count_seq, 1.0)).reshape(1)
    return (seq_kl, unite_grad)


def solution(mesh):
    fine = Mesh(mesh.devices.reshape(4, 2, 4, 2, 2), ALL)
    tensor = ("z", "yl", "c")
    placed = (
        P(None, "x", "yh", tensor),
        P("x", "yh", tensor),
        P(None, tensor, GROUP),
        P(),
        P(tensor, None),
        P("x"),
        P("x", "yh"),
    )
    return jax.shard_map(
        local,
        mesh=fine,
        in_specs=placed,
        out_specs=(P("x"), P(None, tensor, GROUP)),
        check_vma=False,
    )
```

```python
import functools

import jax
import jax.numpy as jnp
from jax import lax
from jax.experimental import pallas as pl
from jax.experimental.pallas import tpu as pltpu
from jax.sharding import Mesh, PartitionSpec as P

NORM_EPS = 1e-05
GROUP = ("x", "yh")
RING = ("z", "yl")
ALL = ("x", "yh", "z", "yl", "c")
GROUPS = 8
HALF = 128
ROWS = 80
SPARE = HALF - ROWS
PIECE = ROWS // 2
MIB = 1 << 20
f32, bf16 = jnp.float32, jnp.bfloat16
SCALARS = pl.BlockSpec(memory_space=pltpu.SMEM)
VECTORS = pl.BlockSpec(memory_space=pltpu.VMEM)
ANYWHERE = pl.BlockSpec(memory_space=pl.ANY)
OWN, X, YH, CORE, TENSOR, HAVE, BLOCKS, SPARES = 0, 1, 2, 3, 4, 5, 8, 16


def spread(value, axes, count):
    return lax.all_to_all(
        jnp.broadcast_to(value[None], (count,) + value.shape), axes, 0, 0, tiled=True
    )


def swap(value, axis, bit, count):
    return lax.ppermute(value, axis, [(i, i ^ bit) for i in range(count)])


def pack_kernel(info_ref, cap_ref, mask_ref, out_ref):
    out_ref[0 : 3 * HALF, :] = cap_ref[...].reshape(3 * HALF, 512)
    lane = lax.broadcasted_iota(jnp.int32, (1, 512), 1)
    masked = (mask_ref[...] == 1).astype(f32)
    near = lax.broadcasted_iota(jnp.int32, (1, HALF), 1) < info_ref[HAVE]
    count = jnp.sum(jnp.where(near, masked, 0.0), axis=1, keepdims=True)
    place = lax.broadcasted_iota(jnp.int32, (HALF, 512), 0) - ROWS
    column = lax.broadcasted_iota(jnp.int32, (HALF, 512), 1)
    tiled = jnp.zeros((HALF, 512), f32)
    for g in range(GROUPS):
        tiled = jnp.where((column - SPARE * g == place) & (place >= 0), 1.0, tiled)
    repeated = jnp.dot(
        jnp.broadcast_to(masked, (8, HALF)).astype(bf16),
        tiled.astype(bf16),
        preferred_element_type=f32,
    )[0:1]
    have = jnp.zeros((1, 512), f32) + info_ref[HAVE].astype(f32)
    row = lax.broadcasted_iota(jnp.int32, (16, 512), 0)
    facts = jnp.where(row == 0, have, jnp.where(row == 1, repeated, 0.0))
    facts = jnp.where(row == 2, count + lane.astype(f32) * 0.0, facts)
    out_ref[3 * HALF : 3 * HALF + 16, :] = facts.astype(bf16)


def pack(info, captured, loss_mask):
    return pl.pallas_call(
        pack_kernel,
        in_specs=[SCALARS, VECTORS, VECTORS],
        out_specs=VECTORS,
        out_shape=jax.ShapeDtypeStruct((3 * HALF + 16, 512), bf16),
        compiler_params=pltpu.CompilerParams(vmem_limit_bytes=8 * MIB),
        name="pack",
    )(info, captured, loss_mask)


def unite_kernel(info_ref, *refs):
    blocks = refs[:GROUPS]
    weight_ref, rows_ref, part_ref, slot_ref, fact_ref, cap_ref, sems = refs[GROUPS:]
    copies = [
        pltpu.make_async_copy(blocks[k], cap_ref.at[info_ref[BLOCKS + k]], sems.at[k])
        for k in range(GROUPS)
    ]
    for copy in copies:
        copy.start()
    for copy in copies:
        copy.wait()
    lane = lax.broadcasted_iota(jnp.int32, (1, 512), 1).astype(f32)
    have, before_more, before_less, facts = [], [], [], []
    more = less = total_count = jnp.zeros((1, 512), f32)
    for g in range(GROUPS):
        fact = cap_ref[g, 3 * HALF : 3 * HALF + 16, :].astype(f32)
        facts.append(fact[1:2])
        have.append(fact[0:1])
        before_more.append(more)
        before_less.append(less)
        more = more + jnp.maximum(have[g] - ROWS, 0.0)
        less = less + jnp.maximum(ROWS - have[g], 0.0)
        total_count = total_count + fact[2:3]
        fact_ref[g : g + 1, :] = fact[2:3, 0:128]
    order = jnp.full((1, 512), -1.0, f32)
    mask_pool = jnp.zeros((1, 512), f32)
    seq_pool = jnp.zeros((1, 512), f32)
    for g in range(GROUPS):
        place = lane - SPARE * g
        mine = (place >= 0) & (place < SPARE)
        order = jnp.where(mine & (place < have[g] - ROWS), before_more[g] + place, order)
        mask_pool = jnp.where(mine, facts[g], mask_pool)
        seq_pool = jnp.where(mine, float(g // 2), seq_pool)
    slot = jnp.full((1, 512), -1.0, f32)
    for g in range(GROUPS):
        offset = order - before_less[g]
        mine = (order >= 0) & (offset >= 0) & (offset < ROWS - have[g])
        slot = jnp.where(mine, ROWS * g + have[g] + offset, slot)
    slot_ref[...] = jnp.concatenate(
        [slot, mask_pool, seq_pool] + [jnp.zeros((1, 512), f32)] * 5, axis=0
    )
    for block in range(2):
        row = lax.broadcasted_iota(jnp.int32, (4 * ROWS, 384), 0) + block * 4 * ROWS
        pick = (row.astype(f32) == slot[:, :384]).astype(bf16)
        total = None
        for s in range(3):
            pool = cap_ref[:, s * HALF + ROWS : (s + 1) * HALF, :].reshape(384, 512)
            moved = jnp.dot(pick, pool, preferred_element_type=f32)
            kept = []
            for g in range(4 * block, 4 * block + 4):
                own = cap_ref[g, s * HALF : s * HALF + ROWS, :].astype(f32)
                within = lax.broadcasted_iota(jnp.int32, (ROWS, 512), 0).astype(f32) < have[g]
                base = (g - 4 * block) * ROWS
                kept.append(jnp.where(within, own, moved[base : base + ROWS]))
            rows = jnp.concatenate(kept, axis=0).astype(bf16)
            rows_ref[s, pl.ds(block * 4 * ROWS, 4 * ROWS), :] = rows
            term = jnp.dot(rows, weight_ref[s], preferred_element_type=f32)
            total = term if total is None else total + term
        for g in range(4):
            for j in range(8):
                for c in range(2):
                    base = g * ROWS + c * PIECE
                    part_ref[4 * block + g, j, c] = total[
                        base : base + PIECE, j * 128 : (j + 1) * 128
                    ].astype(bf16)


def unite(info, blocks, weight):
    return pl.pallas_call(
        unite_kernel,
        in_specs=[SCALARS] + [ANYWHERE] * GROUPS + [VECTORS],
        out_specs=[VECTORS] * 4,
        out_shape=(
            jax.ShapeDtypeStruct((3, GROUPS * ROWS, 512), bf16),
            jax.ShapeDtypeStruct((GROUPS, 8, 2, PIECE, 128), bf16),
            jax.ShapeDtypeStruct((8, 512), f32),
            jax.ShapeDtypeStruct((GROUPS, 128), f32),
        ),
        scratch_shapes=[
            pltpu.VMEM((GROUPS, 3 * HALF + 16, 512), bf16),
            pltpu.SemaphoreType.DMA((GROUPS,)),
        ],
        compiler_params=pltpu.CompilerParams(vmem_limit_bytes=40 * MIB),
        name="unite",
    )(info, *blocks, weight)


def head_kernel(info_ref, own_ref, other_ref, gain_ref, target_ref, mask_ref, slot_ref, *refs):
    spares = refs[:GROUPS]
    head_ref, logit_ref, chosen_ref, stat_ref, side_ref, united_ref = refs[GROUPS : GROUPS + 6]
    wide, normed, held, pool, sems, pool_sems = refs[GROUPS + 6 :]
    width = wide.shape[1]
    tile = head_ref.shape[0] // 4
    loads = [
        pltpu.make_async_copy(
            head_ref.at[pl.ds(i * tile, tile)], held.at[pl.ds(i * tile, tile)], sems.at[i]
        )
        for i in range(4)
    ]
    moves = [
        pltpu.make_async_copy(spares[k], pool.at[info_ref[SPARES + k]], pool_sems.at[k])
        for k in range(GROUPS)
    ]
    for copy in moves + loads:
        copy.start()

    first = info_ref[CORE] == 0
    wide[ROWS:HALF, :] = jnp.zeros((HALF - ROWS, width), f32)
    for g in range(GROUPS):
        for j in range(8):
            column = (g * 8 + j) * 128
            a = own_ref[j, g].astype(f32)
            b = other_ref[j, g].astype(f32)
            wide[0:PIECE, column : column + 128] = jnp.where(first, a, b)
            wide[PIECE:ROWS, column : column + 128] = jnp.where(first, b, a)
    square = jnp.zeros((HALF, 1), f32)
    for g in range(GROUPS):
        values = wide[:, g * 1024 : (g + 1) * 1024]
        square = square + jnp.sum(values * values, axis=1, keepdims=True)
    scale = lax.rsqrt(square / width + NORM_EPS)
    for g in range(GROUPS):
        part = slice(g * 1024, (g + 1) * 1024)
        values = wide[:, part]
        united_ref[:, part] = values[0:ROWS].astype(bf16)
        normed[part, :] = jnp.transpose(values * scale * gain_ref[:, part]).astype(bf16)

    for copy in moves:
        copy.wait()
    have = info_ref[HAVE]
    row = lax.broadcasted_iota(jnp.int32, (HALF, 384), 0) + info_ref[OWN] * ROWS
    pick = (row.astype(f32) == slot_ref[0:1, 0:384]).astype(bf16)
    moved = jnp.dot(pick, pool[...].reshape(384, pool.shape[2]), preferred_element_type=f32)
    kept = lax.broadcasted_iota(jnp.int32, moved.shape, 0) < have
    chosen = jnp.transpose(jnp.where(kept, target_ref[...].astype(f32), moved))
    chosen_ref[...] = chosen
    traits = lax.dot_general(
        slot_ref[:, 0:384].astype(bf16), pick, (((1,), (1,)), ((), ())), preferred_element_type=f32
    )
    lane = lax.broadcasted_iota(jnp.int32, (1, HALF), 1)
    masked = (mask_ref[...] == 1).astype(f32)
    valid = jnp.where(lane < have, masked, traits[1:2])
    valid = jnp.where(lane < ROWS, valid, 0.0)
    sequence = jnp.where(lane < have, info_ref[X].astype(f32), traits[2:3])
    scale_lane = jnp.transpose(jnp.broadcast_to(scale, (HALF, HALF)))[0:1]
    nothing = jnp.zeros((1, HALF), f32)
    side_ref[...] = jnp.concatenate([scale_lane, valid, sequence] + [nothing] * 5, axis=0)

    top_t = jnp.max(chosen, axis=0, keepdims=True)
    pow_t = jnp.exp(chosen - top_t)
    sum_t = jnp.sum(pow_t, axis=0, keepdims=True)
    dot_t = jnp.sum(pow_t * chosen, axis=0, keepdims=True)
    for i in range(4):
        loads[i].wait()
        part = slice(i * tile, (i + 1) * tile)
        logit_ref[part, :] = jnp.dot(held[part, :], normed[...], preferred_element_type=f32)
    logits = logit_ref[...]
    top_d = jnp.max(logits, axis=0, keepdims=True)
    pow_d = jnp.exp(logits - top_d)
    stat_ref[...] = jnp.concatenate(
        [
            top_t,
            sum_t,
            dot_t,
            jnp.sum(pow_t * logits, axis=0, keepdims=True),
            top_d,
            jnp.sum(pow_d, axis=0, keepdims=True),
            jnp.sum(pow_d * logits, axis=0, keepdims=True),
            nothing,
        ],
        axis=0,
    )


def head_forward(info, own, other, gain, target, loss_mask, slots, spares, head):
    vocab, width = head.shape
    return pl.pallas_call(
        head_kernel,
        in_specs=[SCALARS] + [VECTORS] * 6 + [ANYWHERE] * (GROUPS + 1),
        out_specs=[VECTORS] * 5,
        out_shape=(
            jax.ShapeDtypeStruct((vocab, HALF), f32),
            jax.ShapeDtypeStruct((vocab, HALF), f32),
            jax.ShapeDtypeStruct((8, HALF), f32),
            jax.ShapeDtypeStruct((8, HALF), f32),
            jax.ShapeDtypeStruct((ROWS, width), bf16),
        ),
        scratch_shapes=[
            pltpu.VMEM((HALF, width), f32),
            pltpu.VMEM((width, HALF), bf16),
            pltpu.VMEM((vocab, width), bf16),
            pltpu.VMEM((GROUPS, SPARE, vocab), bf16),
            pltpu.SemaphoreType.DMA((4,)),
            pltpu.SemaphoreType.DMA((GROUPS,)),
        ],
        compiler_params=pltpu.CompilerParams(vmem_limit_bytes=44 * MIB),
        name="head_forward",
    )(info, own, other, gain, target, loss_mask, slots, *spares, head)


def back_kernel(
    info_ref, every_ref, logit_ref, chosen_ref, side_ref, gain_ref, united_ref, head_ref,
    out_ref, sum_ref, held, sems,
):
    width = gain_ref.shape[1]
    loads = [
        pltpu.make_async_copy(
            head_ref.at[:, pl.ds(g * 1024, 1024)], held.at[g], sems.at[g]
        )
        for g in range(GROUPS)
    ]
    for copy in loads:
        copy.start()
    every = every_ref[...]
    max_t = jnp.max(every[:, 0:1], axis=0)
    scale_t = jnp.exp(every[:, 0:1] - max_t[None])
    sum_t = jnp.sum(every[:, 1:2] * scale_t, axis=0)
    mean_tt = jnp.sum(every[:, 2:3] * scale_t, axis=0) / sum_t
    mean_tl = jnp.sum(every[:, 3:4] * scale_t, axis=0) / sum_t
    max_d = jnp.max(every[:, 4:5], axis=0)
    scale_d = jnp.exp(every[:, 4:5] - max_d[None])
    sum_d = jnp.sum(every[:, 5:6] * scale_d, axis=0)
    mean_dl = jnp.sum(every[:, 6:7] * scale_d, axis=0) / sum_d
    log_t = max_t + jnp.log(sum_t)
    log_d = max_d + jnp.log(sum_d)
    row_scale, valid, sequence = side_ref[0:1], side_ref[1:2], side_ref[2:3]
    kl = (mean_tt - mean_tl - log_t + log_d) * valid
    row = lax.broadcasted_iota(jnp.int32, (8, HALF), 0)
    sum_ref[...] = jnp.broadcast_to(
        jnp.sum(jnp.where(row.astype(f32) == sequence, kl, 0.0), axis=1, keepdims=True), (8, HALF)
    )

    weight = valid * row_scale
    grad = weight * (jnp.exp(logit_ref[...] - log_d) - jnp.exp(chosen_ref[...] - log_t))
    grad = jnp.transpose(grad)[0:ROWS].astype(bf16)
    lane = lax.broadcasted_iota(jnp.int32, (1, HALF), 1)
    share = ROWS // 16
    mine = (lane >= info_ref[TENSOR] * share) & (lane < (info_ref[TENSOR] + 1) * share)
    cubic = jnp.where(mine, weight * row_scale * (mean_dl - mean_tl) / width, 0.0)
    cubic = jnp.transpose(jnp.broadcast_to(cubic, (HALF, HALF)))[0:ROWS, 0:1]
    for g in range(GROUPS):
        part = slice(g * 1024, (g + 1) * 1024)
        loads[g].wait()
        block = jnp.dot(grad, held[g], preferred_element_type=f32)
        block = block * gain_ref[:, part] - cubic * united_ref[:, part].astype(f32)
        for j in range(8):
            for c in range(2):
                out_ref[g, j, c] = block[
                    c * PIECE : (c + 1) * PIECE, j * 128 : (j + 1) * 128
                ].astype(bf16)


def head_backward(info, every, logits, chosen, side, gain, united, head):
    vocab = head.shape[0]
    return pl.pallas_call(
        back_kernel,
        in_specs=[SCALARS] + [VECTORS] * 6 + [ANYWHERE],
        out_specs=[VECTORS] * 2,
        out_shape=(
            jax.ShapeDtypeStruct((GROUPS, 8, 2, PIECE, 128), bf16),
            jax.ShapeDtypeStruct((8, HALF), f32),
        ),
        scratch_shapes=[
            pltpu.VMEM((GROUPS, vocab, 1024), bf16),
            pltpu.SemaphoreType.DMA((GROUPS,)),
        ],
        compiler_params=pltpu.CompilerParams(vmem_limit_bytes=44 * MIB),
        name="head_backward",
    )(info, every, logits, chosen, side, gain, united, head)


def grad_kernel(core_ref, factor_ref, own_ref, other_ref, rows_ref, out_ref, wide, grads):
    @pl.when((pl.program_id(0) == 0) & (pl.program_id(1) == 0))
    def _():
        first = core_ref[0] == 0
        for g in range(GROUPS):
            for j in range(8):
                a = own_ref[j, g].astype(f32)
                b = other_ref[j, g].astype(f32)
                base = g * ROWS
                wide[base : base + PIECE, j * 128 : (j + 1) * 128] = jnp.where(first, a, b)
                wide[base + PIECE : base + ROWS, j * 128 : (j + 1) * 128] = jnp.where(first, b, a)
        grads[...] = wide[...].astype(bf16)

    out_ref[0] = factor_ref[0] * lax.dot_general(
        rows_ref[0], grads[...], (((0,), (0,)), ((), ())), preferred_element_type=f32
    )


def weight_gradient(core, factor, own, other, rows):
    total = GROUPS * ROWS
    whole = lambda shape: pl.BlockSpec(shape, lambda s, i: (0,) * len(shape))
    return pl.pallas_call(
        grad_kernel,
        grid=(3, 2),
        in_specs=[
            pl.BlockSpec(memory_space=pltpu.SMEM),
            pl.BlockSpec(memory_space=pltpu.SMEM),
            whole((8, GROUPS, PIECE, 128)),
            whole((8, GROUPS, PIECE, 128)),
            pl.BlockSpec((1, total, 256), lambda s, i: (s, 0, i)),
        ],
        out_specs=pl.BlockSpec((1, 256, 1024), lambda s, i: (s, i, 0)),
        out_shape=jax.ShapeDtypeStruct((3, 512, 1024), f32),
        scratch_shapes=[pltpu.VMEM((total, 1024), f32), pltpu.VMEM((total, 1024), bf16)],
        compiler_params=pltpu.CompilerParams(vmem_limit_bytes=40 * MIB),
        name="weight_gradient",
    )(core, factor, own, other, rows)


def sum_over_tensor(pieces):
    received = lax.all_to_all(pieces.reshape(128, PIECE, 128), ALL, 0, 0, tiled=True)
    return jnp.sum(received.reshape(GROUPS, 16, PIECE, 128).astype(f32), axis=1).astype(bf16)


def route(value, first, second):
    moves = {"y": (0, 1), "right": (1, 0), "left": (3, 0), "far": (2, 0)}
    pairs = []
    for x in range(4):
        for y in range(2):
            for c, step in enumerate((first, second)):
                dx, dy = moves[step]
                target = ((x + dx) % 4 * 2 + (y ^ dy)) * 2 + c
                pairs.append(((x * 2 + y) * 2 + c, target))
    return lax.ppermute(value, ("x", "yh", "c"), pairs)


def gather_blocks(own):
    first = lax.axis_index("c") == 0
    r1 = route(own, "y", "right")
    r2 = route(own, "right", "left")
    r3 = route(own, "left", "far")
    r4 = route(own, "far", "y")
    r5 = route(r1, "right", "y")
    r6 = route(jnp.where(first, r1, r2), "left", "y")
    r7 = route(jnp.where(first, r1, r3), "far", "y")
    return [own, r1, r2, r3, r4, r5, r6, r7]


def local(captured, target_logits, unite_weight, norm_gain, head_weight, lengths, loss_mask):
    width = norm_gain.shape[0]
    x, yh, core = lax.axis_index("x"), lax.axis_index("yh"), lax.axis_index("c")
    have = jnp.clip(lengths[0] - yh * HALF, 0, HALF)

    def group_of(dx, dy):
        return (x + dx) % 4 * 2 + (yh ^ dy)

    early = [group_of(0, 1), group_of(3, 0), group_of(1, 0), group_of(2, 0)]
    late = [early[1], early[2], early[3], early[0]]
    offsets = [(dx, dy) for dx in range(4) for dy in range(2)]
    info = jnp.stack(
        [group_of(0, 0), x, yh, core, lax.axis_index(("z", "yl", "c")), have, have, have]
        + [group_of(0, 0)]
        + [jnp.where(core == 0, a, b) for a, b in zip(early, late)]
        + [group_of(3, 1), group_of(1, 1), group_of(2, 1)]
        + [group_of(-dx % 4, dy) for dx, dy in offsets]
    ).astype(jnp.int32)

    blocks = gather_blocks(pack(info, captured.reshape(3, HALF, 512), loss_mask))
    rows, partial, slots, counts = unite(info, blocks, unite_weight)

    target = target_logits.reshape(HALF, -1)
    partial, spare = lax.optimization_barrier((partial, target[ROWS:]))
    spares = [spare]
    for dx, dy in offsets[1:]:
        pairs = [
            (p * 2 + q, (p + dx) % 4 * 2 + (q ^ dy)) for p in range(4) for q in range(2)
        ]
        spares.append(lax.ppermute(spare, GROUP, pairs))

    own_united = spread(sum_over_tensor(partial), RING, 8)
    other_united = swap(own_united, "c", 1, 2)
    gain = norm_gain.reshape(1, width)
    logits, chosen, stats, side, united = head_forward(
        info, own_united, other_united, gain, target, loss_mask, slots, spares, head_weight
    )
    every = spread(stats, ("z", "yl", "c"), 16)
    grad_pieces, seq_sums = head_backward(
        info, every, logits, chosen, side, gain, united, head_weight
    )
    grad_sum = sum_over_tensor(grad_pieces)
    seq_sums = seq_sums + swap(seq_sums, "yh", 1, 2)
    grad_sum, seq_sums = lax.optimization_barrier((grad_sum, seq_sums))
    own_grad = spread(grad_sum, RING, 8)
    seq_sums = seq_sums + swap(seq_sums, "x", 1, 4)
    own_grad, seq_sums = lax.optimization_barrier((own_grad, seq_sums))
    other_grad = swap(own_grad, "c", 1, 2)
    seq_sums = seq_sums + swap(seq_sums, "x", 2, 4)

    counts = counts[:, 0]
    factor = (2 * HALF) / jnp.maximum(jnp.sum(counts), 1.0)
    unite_grad = weight_gradient(core.reshape(1), factor.reshape(1), own_grad, other_grad, rows)
    here = lax.iota(jnp.int32, GROUPS)
    count_seq = jnp.sum(jnp.where(here // 2 == x, counts, 0.0))
    seq_sum = jnp.sum(jnp.where(here == x, seq_sums[:, 0], 0.0))
    seq_kl = (seq_sum / jnp.maximum(count_seq, 1.0)).reshape(1)
    return (seq_kl, unite_grad)


def solution(mesh):
    fine = Mesh(mesh.devices.reshape(4, 2, 4, 2, 2), ALL)
    tensor = ("z", "yl", "c")
    placed = (
        P(None, "x", "yh", tensor),
        P("x", "yh", tensor),
        P(None, tensor, GROUP),
        P(),
        P(tensor, None),
        P("x"),
        P("x", "yh"),
    )
    return jax.shard_map(
        local,
        mesh=fine,
        in_specs=placed,
        out_specs=(P("x"), P(None, tensor, GROUP)),
        check_vma=False,
    )
```

```python
import functools

import jax
import jax.numpy as jnp
from jax import lax
from jax.experimental import pallas as pl
from jax.experimental.pallas import tpu as pltpu
from jax.sharding import Mesh, PartitionSpec as P

NORM_EPS = 1e-05
GROUP = ("x", "yh")
RING = ("z", "yl")
CHIPS = ("x", "yh", "z", "yl")
ALL = CHIPS + ("c",)
OFFSETS = [(dx, dy) for dx in range(4) for dy in range(2)]
GROUPS = 8
HALF = 128
ROWS = 80
SPARE = HALF - ROWS
PIECE = ROWS // 2
MIB = 1 << 20
f32, bf16 = jnp.float32, jnp.bfloat16
SCALARS = pl.BlockSpec(memory_space=pltpu.SMEM)
VECTORS = pl.BlockSpec(memory_space=pltpu.VMEM)
ANYWHERE = pl.BlockSpec(memory_space=pl.ANY)


def group_at(dx, dy):
    return lax.rem(lax.axis_index("x") + dx, 4) * 2 + lax.rem(lax.axis_index("yh") + dy, 2)


def have_here(length):
    return jnp.clip(length - lax.axis_index("yh") * HALF, 0, HALF)


def spread(value, axes, count):
    return lax.all_to_all(
        jnp.broadcast_to(value[None], (count,) + value.shape), axes, 0, 0, tiled=True
    )


def swap(value, axis, bit, count):
    return lax.ppermute(value, axis, [(i, i ^ bit) for i in range(count)])


def pack_kernel(length_ref, cap_ref, mask_ref, out_ref):
    out_ref[0 : 3 * HALF, :] = cap_ref[...].reshape(3 * HALF, 512)
    lane = lax.broadcasted_iota(jnp.int32, (1, 512), 1)
    masked = (mask_ref[...] == 1).astype(f32)
    here = have_here(length_ref[0])
    near = lax.broadcasted_iota(jnp.int32, (1, HALF), 1) < here
    count = jnp.sum(jnp.where(near, masked, 0.0), axis=1, keepdims=True)
    place = lax.broadcasted_iota(jnp.int32, (HALF, 512), 0) - ROWS
    column = lax.broadcasted_iota(jnp.int32, (HALF, 512), 1)
    tiled = jnp.zeros((HALF, 512), f32)
    for g in range(GROUPS):
        tiled = jnp.where((column - SPARE * g == place) & (place >= 0), 1.0, tiled)
    repeated = jnp.dot(
        jnp.broadcast_to(masked, (8, HALF)).astype(bf16),
        tiled.astype(bf16),
        preferred_element_type=f32,
    )[0:1]
    have = jnp.zeros((1, 512), f32) + here.astype(f32)
    row = lax.broadcasted_iota(jnp.int32, (16, 512), 0)
    facts = jnp.where(row == 0, have, jnp.where(row == 1, repeated, 0.0))
    facts = jnp.where(row == 2, count + lane.astype(f32) * 0.0, facts)
    out_ref[3 * HALF : 3 * HALF + 16, :] = facts.astype(bf16)


def pack(lengths, captured, loss_mask):
    return pl.pallas_call(
        pack_kernel,
        in_specs=[SCALARS, VECTORS, VECTORS],
        out_specs=VECTORS,
        out_shape=jax.ShapeDtypeStruct((3 * HALF + 16, 512), bf16),
        compiler_params=pltpu.CompilerParams(vmem_limit_bytes=8 * MIB),
        name="pack",
    )(lengths, captured, loss_mask)


def split_by_core(block, first, mine_ref, other_ref, extra=None):
    for j in range(8):
        upper = block[0:PIECE, j * 128 : (j + 1) * 128]
        lower = block[PIECE:ROWS, j * 128 : (j + 1) * 128]
        mine = jnp.where(first, upper, lower)
        other = jnp.where(first, lower, upper)
        if extra is not None:
            mine = jnp.concatenate([mine, extra], axis=0)
            other = jnp.concatenate([other, jnp.zeros_like(extra)], axis=0)
        mine_ref[j] = mine.astype(bf16)
        other_ref[j] = other.astype(bf16)


def unite_kernel(*refs):
    blocks = refs[:GROUPS]
    hbm_weight, rows_ref, mine_ref, other_ref, slot_ref, fact_ref, cap_ref, weight_ref, sems = refs[
        GROUPS:
    ]
    core = lax.axis_index("c")
    places = [(0, 0), (0, 1), (3, 0), (1, 0), (2, 0), (3, 1), (1, 1), (2, 1)]
    copies = [
        pltpu.make_async_copy(block, cap_ref.at[group_at(*place)], sems.at[k])
        for k, (block, place) in enumerate(zip(blocks, places))
    ]
    loads = [
        pltpu.make_async_copy(hbm_weight.at[k], weight_ref.at[k], sems.at[GROUPS + k])
        for k in range(3)
    ]
    for copy in copies + loads:
        copy.start()
    for copy in copies:
        copy.wait()
    lane = lax.broadcasted_iota(jnp.int32, (1, 512), 1).astype(f32)
    have, before_more, before_less, facts = [], [], [], []
    more = less = total_count = jnp.zeros((1, 512), f32)
    for g in range(GROUPS):
        fact = cap_ref[g, 3 * HALF : 3 * HALF + 16, :].astype(f32)
        facts.append(fact[1:2])
        have.append(fact[0:1])
        before_more.append(more)
        before_less.append(less)
        more = more + jnp.maximum(have[g] - ROWS, 0.0)
        less = less + jnp.maximum(ROWS - have[g], 0.0)
        total_count = total_count + fact[2:3]
        fact_ref[g : g + 1, :] = fact[2:3, 0:128]
    order = jnp.full((1, 512), -1.0, f32)
    mask_pool = jnp.zeros((1, 512), f32)
    seq_pool = jnp.zeros((1, 512), f32)
    for g in range(GROUPS):
        place = lane - SPARE * g
        mine = (place >= 0) & (place < SPARE)
        order = jnp.where(mine & (place < have[g] - ROWS), before_more[g] + place, order)
        mask_pool = jnp.where(mine, facts[g], mask_pool)
        seq_pool = jnp.where(mine, float(g // 2), seq_pool)
    slot = jnp.full((1, 512), -1.0, f32)
    for g in range(GROUPS):
        offset = order - before_less[g]
        mine = (order >= 0) & (offset >= 0) & (offset < ROWS - have[g])
        slot = jnp.where(mine, ROWS * g + have[g] + offset, slot)
    slot_ref[...] = jnp.concatenate(
        [slot, mask_pool, seq_pool] + [jnp.zeros((1, 512), f32)] * 5, axis=0
    )
    for block in range(2):
        row = lax.broadcasted_iota(jnp.int32, (4 * ROWS, 384), 0) + block * 4 * ROWS
        pick = (row.astype(f32) == slot[:, :384]).astype(bf16)
        total = None
        for s in range(3):
            pool = cap_ref[:, s * HALF + ROWS : (s + 1) * HALF, :].reshape(384, 512)
            moved = jnp.dot(pick, pool, preferred_element_type=f32)
            kept = []
            for g in range(4 * block, 4 * block + 4):
                own = cap_ref[g, s * HALF : s * HALF + ROWS, :].astype(f32)
                within = lax.broadcasted_iota(jnp.int32, (ROWS, 512), 0).astype(f32) < have[g]
                base = (g - 4 * block) * ROWS
                kept.append(jnp.where(within, own, moved[base : base + ROWS]))
            rows = jnp.concatenate(kept, axis=0).astype(bf16)
            rows_ref[s, pl.ds(block * 4 * ROWS, 4 * ROWS), :] = rows
            if block == 0:
                loads[s].wait()
            term = jnp.dot(rows, weight_ref[s], preferred_element_type=f32)
            total = term if total is None else total + term
        for g in range(4):
            base = g * ROWS
            split_by_core(
                total[base : base + ROWS], core == 0, mine_ref.at[4 * block + g], other_ref.at[4 * block + g]
            )


def unite(blocks, weight):
    return pl.pallas_call(
        unite_kernel,
        in_specs=[ANYWHERE] * (GROUPS + 1),
        out_specs=[VECTORS] * 5,
        out_shape=(
            jax.ShapeDtypeStruct((3, GROUPS * ROWS, 512), bf16),
            jax.ShapeDtypeStruct((GROUPS, 8, PIECE, 128), bf16),
            jax.ShapeDtypeStruct((GROUPS, 8, PIECE, 128), bf16),
            jax.ShapeDtypeStruct((8, 512), f32),
            jax.ShapeDtypeStruct((GROUPS, 128), f32),
        ),
        scratch_shapes=[
            pltpu.VMEM((GROUPS, 3 * HALF + 16, 512), bf16),
            pltpu.VMEM(weight.shape, bf16),
            pltpu.SemaphoreType.DMA((GROUPS + 3,)),
        ],
        compiler_params=pltpu.CompilerParams(vmem_limit_bytes=52 * MIB),
        name="unite",
    )(*blocks, weight)


def head_kernel(length_ref, own_ref, other_ref, gain_ref, target_ref, mask_ref, slot_ref, *refs):
    spares = refs[:4]
    head_ref, logit_ref, chosen_ref, stat_ref, side_ref, united_ref = refs[4:10]
    wide, normed, held, pool, sems, pool_sems = refs[10:]
    width = wide.shape[1]
    tile = head_ref.shape[0] // 8
    loads = [
        pltpu.make_async_copy(
            head_ref.at[pl.ds(i * tile, tile)], held.at[pl.ds(i * tile, tile)], sems.at[i]
        )
        for i in range(8)
    ]
    moves = [
        pltpu.make_async_copy(spares[dx].at[dy], pool.at[group_at(-dx % 4, dy)], pool_sems.at[k])
        for k, (dx, dy) in enumerate(OFFSETS)
    ]
    for copy in moves + loads[:3]:
        copy.start()

    first = lax.axis_index("c") == 0
    wide[ROWS:HALF, :] = jnp.zeros((HALF - ROWS, width), f32)
    for g in range(GROUPS):
        for j in range(8):
            column = (g * 8 + j) * 128
            a = own_ref[j, g].astype(f32)
            b = other_ref[j, g].astype(f32)
            wide[0:PIECE, column : column + 128] = jnp.where(first, a, b)
            wide[PIECE:ROWS, column : column + 128] = jnp.where(first, b, a)
    square = jnp.zeros((HALF, 1), f32)
    for g in range(GROUPS):
        values = wide[:, g * 1024 : (g + 1) * 1024]
        square = square + jnp.sum(values * values, axis=1, keepdims=True)
    scale = lax.rsqrt(square / width + NORM_EPS)
    for g in range(GROUPS):
        part = slice(g * 1024, (g + 1) * 1024)
        values = wide[:, part]
        united_ref[:, part] = values[0:ROWS].astype(bf16)
        normed[part, :] = jnp.transpose(values * scale * gain_ref[:, part]).astype(bf16)

    for copy in moves:
        copy.wait()
    have = have_here(length_ref[0])
    row = lax.broadcasted_iota(jnp.int32, (HALF, 384), 0) + group_at(0, 0) * ROWS
    pick = (row.astype(f32) == slot_ref[0:1, 0:384]).astype(bf16)
    moved = jnp.dot(pick, pool[...].reshape(384, pool.shape[2]), preferred_element_type=f32)
    kept = lax.broadcasted_iota(jnp.int32, moved.shape, 0) < have
    chosen = jnp.transpose(jnp.where(kept, target_ref[...].astype(f32), moved))
    chosen_ref[...] = chosen
    traits = lax.dot_general(
        slot_ref[:, 0:384].astype(bf16), pick, (((1,), (1,)), ((), ())), preferred_element_type=f32
    )
    lane = lax.broadcasted_iota(jnp.int32, (1, HALF), 1)
    masked = (mask_ref[...] == 1).astype(f32)
    valid = jnp.where(lane < have, masked, traits[1:2])
    valid = jnp.where(lane < ROWS, valid, 0.0)
    sequence = jnp.where(lane < have, lax.axis_index("x").astype(f32), traits[2:3])
    scale_lane = jnp.transpose(jnp.broadcast_to(scale, (HALF, HALF)))[0:1]
    nothing = jnp.zeros((1, HALF), f32)
    side_ref[...] = jnp.concatenate([scale_lane, valid, sequence] + [nothing] * 5, axis=0)

    top_t = jnp.max(chosen, axis=0, keepdims=True)
    pow_t = jnp.exp(chosen - top_t)
    sum_t = jnp.sum(pow_t, axis=0, keepdims=True)
    dot_t = jnp.sum(pow_t * chosen, axis=0, keepdims=True)
    for i in range(0, 8, 2):
        for k in (i, i + 1):
            loads[k].wait()
            if k + 3 < 8:
                loads[k + 3].start()
        part = slice(i * tile, (i + 2) * tile)
        logit_ref[part, :] = jnp.dot(held[part, :], normed[...], preferred_element_type=f32)
    logits = logit_ref[...]
    top_d = jnp.max(logits, axis=0, keepdims=True)
    pow_d = jnp.exp(logits - top_d)
    stat_ref[...] = jnp.concatenate(
        [
            top_t,
            sum_t,
            dot_t,
            jnp.sum(pow_t * logits, axis=0, keepdims=True),
            top_d,
            jnp.sum(pow_d, axis=0, keepdims=True),
            jnp.sum(pow_d * logits, axis=0, keepdims=True),
            nothing,
        ],
        axis=0,
    )


def head_forward(lengths, own, other, gain, target, loss_mask, slots, spares, head):
    vocab, width = head.shape
    return pl.pallas_call(
        head_kernel,
        in_specs=[SCALARS] + [VECTORS] * 6 + [ANYWHERE] * 5,
        out_specs=[VECTORS] * 5,
        out_shape=(
            jax.ShapeDtypeStruct((vocab, HALF), f32),
            jax.ShapeDtypeStruct((vocab, HALF), f32),
            jax.ShapeDtypeStruct((8, HALF), f32),
            jax.ShapeDtypeStruct((8, HALF), f32),
            jax.ShapeDtypeStruct((ROWS, width), bf16),
        ),
        scratch_shapes=[
            pltpu.VMEM((HALF, width), f32),
            pltpu.VMEM((width, HALF), bf16),
            pltpu.VMEM((vocab, width), bf16),
            pltpu.VMEM((GROUPS, SPARE, vocab), bf16),
            pltpu.SemaphoreType.DMA((8,)),
            pltpu.SemaphoreType.DMA((GROUPS,)),
        ],
        compiler_params=pltpu.CompilerParams(vmem_limit_bytes=44 * MIB),
        name="head_forward",
    )(lengths, own, other, gain, target, loss_mask, slots, *spares, head)


def back_kernel(
    every_ref, logit_ref, chosen_ref, side_ref, gain_ref, united_ref, head_ref,
    mine_ref, other_ref, held, sems,
):
    width = gain_ref.shape[1]
    loads = [
        pltpu.make_async_copy(
            head_ref.at[:, pl.ds(g * 1024, 1024)], held.at[g], sems.at[g]
        )
        for g in range(GROUPS)
    ]
    for copy in loads[:3]:
        copy.start()
    every = every_ref[...]
    max_t = jnp.max(every[:, 0:1], axis=0)
    scale_t = jnp.exp(every[:, 0:1] - max_t[None])
    sum_t = jnp.sum(every[:, 1:2] * scale_t, axis=0)
    mean_tt = jnp.sum(every[:, 2:3] * scale_t, axis=0) / sum_t
    mean_tl = jnp.sum(every[:, 3:4] * scale_t, axis=0) / sum_t
    max_d = jnp.max(every[:, 4:5], axis=0)
    scale_d = jnp.exp(every[:, 4:5] - max_d[None])
    sum_d = jnp.sum(every[:, 5:6] * scale_d, axis=0)
    mean_dl = jnp.sum(every[:, 6:7] * scale_d, axis=0) / sum_d
    log_t = max_t + jnp.log(sum_t)
    log_d = max_d + jnp.log(sum_d)
    row_scale, valid, sequence = side_ref[0:1], side_ref[1:2], side_ref[2:3]
    kl = (mean_tt - mean_tl - log_t + log_d) * valid
    row = lax.broadcasted_iota(jnp.int32, (8, HALF), 0)
    sums = jnp.sum(jnp.where(row.astype(f32) == sequence, kl, 0.0), axis=1, keepdims=True)
    sums = jnp.broadcast_to(sums, (8, HALF))
    high = sums.astype(bf16).astype(f32)
    middle = (sums - high).astype(bf16).astype(f32)
    column = lax.broadcasted_iota(jnp.int32, (8, HALF), 1)
    third = jnp.where(column < 96, sums - high - middle, 0.0)
    sums = jnp.where(column < 32, high, jnp.where(column < 64, middle, third))

    weight = valid * row_scale
    grad = weight * (jnp.exp(logit_ref[...] - log_d) - jnp.exp(chosen_ref[...] - log_t))
    grad = jnp.transpose(grad)[0:ROWS].astype(bf16)
    lane = lax.broadcasted_iota(jnp.int32, (1, HALF), 1)
    share = ROWS // 16
    index = lax.axis_index(("z", "yl", "c"))
    mine = (lane >= index * share) & (lane < (index + 1) * share)
    cubic = jnp.where(mine, weight * row_scale * (mean_dl - mean_tl) / width, 0.0)
    cubic = jnp.transpose(jnp.broadcast_to(cubic, (HALF, HALF)))[0:ROWS, 0:1]
    for g in range(GROUPS):
        part = slice(g * 1024, (g + 1) * 1024)
        loads[g].wait()
        if g + 3 < GROUPS:
            loads[g + 3].start()
        block = jnp.dot(grad, held[g], preferred_element_type=f32)
        block = block * gain_ref[:, part] - cubic * united_ref[:, part].astype(f32)
        split_by_core(
            block, lax.axis_index("c") == 0, mine_ref.at[g], other_ref.at[g], sums
        )


def head_backward(every, logits, chosen, side, gain, united, head):
    vocab = head.shape[0]
    return pl.pallas_call(
        back_kernel,
        in_specs=[VECTORS] * 6 + [ANYWHERE],
        out_specs=[VECTORS] * 2,
        out_shape=(
            jax.ShapeDtypeStruct((GROUPS, 8, PIECE + 8, 128), bf16),
            jax.ShapeDtypeStruct((GROUPS, 8, PIECE + 8, 128), bf16),
        ),
        scratch_shapes=[
            pltpu.VMEM((GROUPS, vocab, 1024), bf16),
            pltpu.SemaphoreType.DMA((GROUPS,)),
        ],
        compiler_params=pltpu.CompilerParams(vmem_limit_bytes=44 * MIB),
        name="head_backward",
    )(every, logits, chosen, side, gain, united, head)


def grad_kernel(factor_ref, own_ref, other_ref, rows_ref, out_ref, wide, grads):
    @pl.when((pl.program_id(0) == 0) & (pl.program_id(1) == 0))
    def _():
        first = lax.axis_index("c") == 0
        for g in range(GROUPS):
            for j in range(8):
                a = own_ref[j, g].astype(f32)
                b = other_ref[j, g].astype(f32)
                base = g * ROWS
                wide[base : base + PIECE, j * 128 : (j + 1) * 128] = jnp.where(first, a, b)
                wide[base + PIECE : base + ROWS, j * 128 : (j + 1) * 128] = jnp.where(first, b, a)
        grads[...] = wide[...].astype(bf16)

    out_ref[0] = factor_ref[0] * lax.dot_general(
        rows_ref[0], grads[...], (((0,), (0,)), ((), ())), preferred_element_type=f32
    )


def weight_gradient(factor, own, other, rows):
    total = GROUPS * ROWS
    whole = lambda shape: pl.BlockSpec(shape, lambda s, i: (0,) * len(shape))
    return pl.pallas_call(
        grad_kernel,
        grid=(3, 2),
        in_specs=[
            SCALARS,
            whole((8, GROUPS, PIECE, 128)),
            whole((8, GROUPS, PIECE, 128)),
            pl.BlockSpec((1, total, 256), lambda s, i: (s, 0, i)),
        ],
        out_specs=pl.BlockSpec((1, 256, 1024), lambda s, i: (s, i, 0)),
        out_shape=jax.ShapeDtypeStruct((3, 512, 1024), f32),
        scratch_shapes=[pltpu.VMEM((total, 1024), f32), pltpu.VMEM((total, 1024), bf16)],
        compiler_params=pltpu.CompilerParams(vmem_limit_bytes=40 * MIB),
        name="weight_gradient",
    )(factor, own, other, rows)


def sum_kernel(piece_ref, out_ref, extra_ref):
    extra = jnp.zeros((8, 128), f32)
    for g in range(GROUPS):
        total = jnp.zeros((PIECE, 128), f32)
        for j in range(8):
            total = total + piece_ref[g * 8 + j, 0:PIECE, :].astype(f32)
        for k in range(8):
            out_ref[k, g] = total.astype(bf16)
        if piece_ref.shape[1] > PIECE:
            extra = extra + piece_ref[g * 8].astype(f32)[PIECE : PIECE + 8]
    extra_ref[...] = extra


def gather_sum(mine, other):
    pair = (mine.astype(f32) + swap(other, "c", 1, 2).astype(f32)).astype(bf16)
    received = lax.all_to_all(pair.reshape((64,) + pair.shape[2:]), CHIPS, 0, 0, tiled=True)
    copies, extra = pl.pallas_call(
        sum_kernel,
        in_specs=[VECTORS],
        out_specs=[VECTORS] * 2,
        out_shape=(
            jax.ShapeDtypeStruct((8, GROUPS, PIECE, 128), bf16),
            jax.ShapeDtypeStruct((8, 128), f32),
        ),
        compiler_params=pltpu.CompilerParams(vmem_limit_bytes=8 * MIB),
        name="sum_pieces",
    )(received)
    return copies, extra


def route(value, dx, dy):
    pairs = [(p * 2 + q, (p + dx) % 4 * 2 + (q ^ dy)) for p in range(4) for q in range(2)]
    return lax.ppermute(value, GROUP, pairs)


def gather_blocks(own):
    far = route(own, 2, 0)
    over = route(own, 0, 1)
    right = route(own, 3, 0)
    left = route(own, 1, 0)
    over_far = route(far, 0, 1)
    over_right = route(over, 3, 0)
    over_left = route(over, 1, 0)
    return [own, over, left, right, far, over_left, over_right, over_far]


def local(captured, target_logits, unite_weight, norm_gain, head_weight, lengths, loss_mask):
    width = norm_gain.shape[0]
    blocks = gather_blocks(pack(lengths, captured.reshape(3, HALF, 512), loss_mask))
    rows, mine, other, slots, counts = unite(blocks, unite_weight)

    target = target_logits.reshape(HALF, -1)
    spare = target[ROWS:]
    pair = jnp.stack([spare, route(spare, 0, 1)])
    mine, pair = lax.optimization_barrier((mine, pair))
    spares = [pair] + [route(pair, dx, 0) for dx in range(1, 4)]
    copies, _ = gather_sum(mine, other)
    copies, *spares = lax.optimization_barrier((copies, *spares))
    own_united = lax.all_to_all(copies, RING, 0, 0, tiled=True)
    other_united = swap(own_united, "c", 1, 2)
    gain = norm_gain.reshape(1, width)
    logits, chosen, stats, side, united = head_forward(
        lengths, own_united, other_united, gain, target, loss_mask, slots, spares, head_weight
    )
    every = spread(stats, ("z", "yl", "c"), 16)
    mine, other = head_backward(every, logits, chosen, side, gain, united, head_weight)
    copies, sums = gather_sum(mine, other)
    own_grad = lax.all_to_all(copies, RING, 0, 0, tiled=True)
    x = lax.axis_index("x")
    counts = counts[:, 0]
    factor = (2 * HALF) / jnp.maximum(jnp.sum(counts), 1.0)
    here = lax.iota(jnp.int32, GROUPS)
    count_seq = jnp.sum(jnp.where(here // 2 == x, counts, 0.0))
    seq_sum = jnp.sum(jnp.where(here[:, None] == x, sums, 0.0)) / 32.0
    seq_kl = (seq_sum / jnp.maximum(count_seq, 1.0)).reshape(1)
    own_grad, seq_kl, factor = lax.optimization_barrier((own_grad, seq_kl, factor))
    other_grad = swap(own_grad, "c", 1, 2)
    unite_grad = weight_gradient(factor.reshape(1), own_grad, other_grad, rows)
    return (seq_kl, unite_grad)


def solution(mesh):
    fine = Mesh(mesh.devices.reshape(4, 2, 4, 2, 2), ALL)
    tensor = ("z", "yl", "c")
    placed = (
        P(None, "x", "yh", tensor),
        P("x", "yh", tensor),
        P(None, tensor, GROUP),
        P(),
        P(tensor, None),
        P("x"),
        P("x", "yh"),
    )
    return jax.shard_map(
        local,
        mesh=fine,
        in_specs=placed,
        out_specs=(P("x"), P(None, tensor, GROUP)),
        check_vma=False,
    )
```

```python
import functools

import jax
import jax.numpy as jnp
from jax import lax
from jax.experimental import pallas as pl
from jax.experimental.pallas import tpu as pltpu
from jax.sharding import Mesh, PartitionSpec as P

NORM_EPS = 1e-05
GROUP = ("x", "yh")
RING = ("z", "yl")
CHIPS = ("x", "yh", "z", "yl")
ALL = CHIPS + ("c",)
PLACES = [(0, 0), (0, 1), (3, 0), (1, 0), (2, 0), (3, 1), (1, 1), (2, 1)]
GROUPS = 8
HALF = 128
ROWS = 80
SPARE = HALF - ROWS
PIECE = ROWS // 2
MIB = 1 << 20
f32, bf16 = jnp.float32, jnp.bfloat16
SCALARS = pl.BlockSpec(memory_space=pltpu.SMEM)
VECTORS = pl.BlockSpec(memory_space=pltpu.VMEM)
FAR = pl.BlockSpec(memory_space=pltpu.HBM)


def group_at(dx, dy):
    return lax.rem(lax.axis_index("x") + dx, 4) * 2 + lax.rem(lax.axis_index("yh") + dy, 2)


def have_here(length):
    return jnp.clip(length - lax.axis_index("yh") * HALF, 0, HALF)


def spread(value, axes, count):
    return lax.all_to_all(
        jnp.broadcast_to(value[None], (count,) + value.shape), axes, 0, 0, tiled=True
    )


def swap(value, axis, bit, count):
    return lax.ppermute(value, axis, [(i, i ^ bit) for i in range(count)])


def spare_kernel(length_ref, mask_ref, target_ref, spare_ref):
    vocab = target_ref.shape[1]
    masked = (mask_ref[...] == 1).astype(f32)
    near = lax.broadcasted_iota(jnp.int32, (1, HALF), 1) < have_here(length_ref[0])
    count = jnp.sum(jnp.where(near, masked, 0.0), axis=1, keepdims=True)
    place = lax.broadcasted_iota(jnp.int32, (HALF, vocab), 0) - ROWS
    column = lax.broadcasted_iota(jnp.int32, (HALF, vocab), 1)
    tiled = jnp.zeros((HALF, vocab), f32)
    for k in range(GROUPS):
        tiled = jnp.where((column - SPARE * k == place) & (place >= 0), 1.0, tiled)
    repeated = jnp.dot(
        jnp.broadcast_to(masked, (8, HALF)).astype(bf16),
        tiled.astype(bf16),
        preferred_element_type=f32,
    )[0:1]
    row = lax.broadcasted_iota(jnp.int32, (16, vocab), 0)
    facts = jnp.where(row == 0, repeated, jnp.where(row == 1, count, 0.0))
    spare_ref[0:SPARE, :] = target_ref[ROWS:HALF, :]
    spare_ref[SPARE : SPARE + 16, :] = facts.astype(bf16)


def spare_facts(lengths, loss_mask, target):
    return pl.pallas_call(
        spare_kernel,
        in_specs=[SCALARS, VECTORS, VECTORS],
        out_specs=VECTORS,
        out_shape=jax.ShapeDtypeStruct((SPARE + 16, target.shape[1]), bf16),
        compiler_params=pltpu.CompilerParams(vmem_limit_bytes=8 * MIB),
        name="spare_facts",
    )(lengths, loss_mask, target)


def stage_kernel(hbm_weight, hbm_cap, weight_ref, cap_ref, sems):
    copies = [
        pltpu.make_async_copy(hbm_weight, weight_ref, sems.at[0]),
        pltpu.make_async_copy(hbm_cap, cap_ref, sems.at[1]),
    ]
    for copy in copies:
        copy.start()
    for copy in copies:
        copy.wait()


def stage(weight, captured):
    return pl.pallas_call(
        stage_kernel,
        in_specs=[FAR, FAR],
        out_specs=[VECTORS] * 2,
        out_shape=(
            jax.ShapeDtypeStruct(weight.shape, bf16),
            jax.ShapeDtypeStruct(captured.shape, bf16),
        ),
        scratch_shapes=[pltpu.SemaphoreType.DMA((2,))],
        compiler_params=pltpu.CompilerParams(vmem_limit_bytes=8 * MIB),
        name="stage",
    )(weight, captured)


def split_by_core(block, first, mine_ref, other_ref, extra=None):
    for j in range(8):
        upper = block[0:PIECE, j * 128 : (j + 1) * 128]
        lower = block[PIECE:ROWS, j * 128 : (j + 1) * 128]
        mine = jnp.where(first, upper, lower)
        other = jnp.where(first, lower, upper)
        if extra is not None:
            mine = jnp.concatenate([mine, extra], axis=0)
            other = jnp.concatenate([other, jnp.zeros_like(extra)], axis=0)
        mine_ref[j] = mine.astype(bf16)
        other_ref[j] = other.astype(bf16)


def unite_kernel(*refs):
    blocks, length_refs = refs[:GROUPS], refs[GROUPS : GROUPS + 4]
    weight_ref, rows_ref, mine_ref, other_ref, slot_ref = refs[GROUPS + 4 :]
    first = lax.axis_index("c") == 0
    groups = [group_at(*place) for place in PLACES]
    lane = lax.broadcasted_iota(jnp.int32, (1, 512), 1).astype(f32)
    have = [
        jnp.clip(
            jnp.broadcast_to(length_refs[-dx % 4][0:1, 0:1], (1, 512))
            - lax.rem(lax.axis_index("yh") + dy, 2).astype(f32) * HALF,
            0.0,
            float(HALF),
        )
        for dx, dy in PLACES
    ]
    more = [jnp.maximum(h - ROWS, 0.0) for h in have]
    less = [jnp.maximum(ROWS - h, 0.0) for h in have]

    def before(amounts, k):
        total = jnp.zeros((1, 512), f32)
        for m in range(GROUPS):
            if m != k:
                total = total + amounts[m] * (groups[m] < groups[k]).astype(f32)
        return total

    order = jnp.full((1, 512), -1.0, f32)
    for k in range(GROUPS):
        place = lane - SPARE * k
        mine = (place >= 0) & (place < SPARE)
        order = jnp.where(mine & (place < have[k] - ROWS), before(more, k) + place, order)
    slot = jnp.full((1, 512), -1.0, f32)
    for k in range(GROUPS):
        offset = order - before(less, k)
        mine = (order >= 0) & (offset >= 0) & (offset < ROWS - have[k])
        slot = jnp.where(mine, ROWS * k + have[k] + offset, slot)
    slot_ref[...] = jnp.broadcast_to(slot, (8, 512))
    for half in range(2):
        row = lax.broadcasted_iota(jnp.int32, (4 * ROWS, 384), 0) + half * 4 * ROWS
        pick = (row.astype(f32) == slot[:, :384]).astype(bf16)
        total = None
        for s in range(3):
            pool = jnp.concatenate([block[s, ROWS:HALF, :] for block in blocks], axis=0)
            moved = jnp.dot(pick, pool, preferred_element_type=f32)
            kept = []
            for k in range(4 * half, 4 * half + 4):
                own = blocks[k][s, 0:ROWS, :].astype(f32)
                within = lax.broadcasted_iota(jnp.int32, (ROWS, 512), 0).astype(f32) < have[k]
                base = (k - 4 * half) * ROWS
                kept.append(jnp.where(within, own, moved[base : base + ROWS]))
            rows = jnp.concatenate(kept, axis=0).astype(bf16)
            rows_ref[s, pl.ds(half * 4 * ROWS, 4 * ROWS), :] = rows
            term = jnp.dot(rows, weight_ref[s], preferred_element_type=f32)
            total = term if total is None else total + term
        for k in range(4):
            group = groups[4 * half + k]
            split_by_core(
                total[k * ROWS : (k + 1) * ROWS], first, mine_ref.at[group], other_ref.at[group]
            )


def unite(blocks, lengths, weight):
    return pl.pallas_call(
        unite_kernel,
        in_specs=[VECTORS] * (GROUPS + 5),
        out_specs=[VECTORS] * 4,
        out_shape=(
            jax.ShapeDtypeStruct((3, GROUPS * ROWS, 512), bf16),
            jax.ShapeDtypeStruct((GROUPS, 8, PIECE, 128), bf16),
            jax.ShapeDtypeStruct((GROUPS, 8, PIECE, 128), bf16),
            jax.ShapeDtypeStruct((8, 512), f32),
        ),
        compiler_params=pltpu.CompilerParams(vmem_limit_bytes=24 * MIB),
        name="unite",
    )(*blocks, *lengths, weight)


def head_kernel(
    own_ref, other_ref, gain_ref, head_ref,
    logit_ref, scale_ref, united_ref, held, wide, normed, sems,
):
    width = wide.shape[1]
    tile = head_ref.shape[0] // 8
    loads = [
        pltpu.make_async_copy(
            head_ref.at[pl.ds(i * tile, tile)], held.at[pl.ds(i * tile, tile)], sems.at[i]
        )
        for i in range(8)
    ]
    for copy in loads[:3]:
        copy.start()

    first = lax.axis_index("c") == 0
    wide[ROWS:HALF, :] = jnp.zeros((HALF - ROWS, width), f32)
    for g in range(GROUPS):
        for j in range(8):
            column = (g * 8 + j) * 128
            a = own_ref[j, g].astype(f32)
            b = other_ref[j, g].astype(f32)
            wide[0:PIECE, column : column + 128] = jnp.where(first, a, b)
            wide[PIECE:ROWS, column : column + 128] = jnp.where(first, b, a)
    square = jnp.zeros((HALF, 1), f32)
    for g in range(GROUPS):
        values = wide[:, g * 1024 : (g + 1) * 1024]
        square = square + jnp.sum(values * values, axis=1, keepdims=True)
    scale = lax.rsqrt(square / width + NORM_EPS)
    for g in range(GROUPS):
        part = slice(g * 1024, (g + 1) * 1024)
        values = wide[:, part]
        united_ref[:, part] = values[0:ROWS].astype(bf16)
        normed[part, :] = jnp.transpose(values * scale * gain_ref[:, part]).astype(bf16)

    scale_ref[...] = jnp.transpose(jnp.broadcast_to(scale, (HALF, HALF)))[0:8]
    for i in range(0, 8, 2):
        for k in (i, i + 1):
            loads[k].wait()
            if k + 3 < 8:
                loads[k + 3].start()
        part = slice(i * tile, (i + 2) * tile)
        logit_ref[part, :] = jnp.dot(held[part, :], normed[...], preferred_element_type=f32)


def head_forward(own, other, gain, head):
    vocab, width = head.shape
    return pl.pallas_call(
        head_kernel,
        in_specs=[VECTORS] * 3 + [FAR],
        out_specs=[VECTORS] * 4,
        out_shape=(
            jax.ShapeDtypeStruct((vocab, HALF), f32),
            jax.ShapeDtypeStruct((8, HALF), f32),
            jax.ShapeDtypeStruct((ROWS, width), bf16),
            jax.ShapeDtypeStruct((vocab, width), bf16),
        ),
        scratch_shapes=[
            pltpu.VMEM((HALF, width), f32),
            pltpu.VMEM((width, HALF), bf16),
            pltpu.SemaphoreType.DMA((8,)),
        ],
        compiler_params=pltpu.CompilerParams(vmem_limit_bytes=24 * MIB),
        cost_estimate=pl.CostEstimate(
            flops=4 * HALF * vocab * width, bytes_accessed=2 * vocab * width, transcendentals=0
        ),
        name="head_forward",
    )(own, other, gain, head)


def stat_kernel(
    length_ref, logit_ref, scale_ref, target_ref, mask_ref, slot_ref, *refs
):
    spares = refs[:4]
    chosen_ref, stat_ref, side_ref, pool, pool_sems = refs[4:]
    moves = [
        pltpu.make_async_copy(spares[-dx % 4].at[dy], pool.at[k], pool_sems.at[k])
        for k, (dx, dy) in enumerate(PLACES)
    ]
    for copy in moves:
        copy.start()
    for copy in moves:
        copy.wait()
    have = have_here(length_ref[0])
    row = lax.broadcasted_iota(jnp.int32, (HALF, 384), 0)
    pick = (row.astype(f32) == slot_ref[0:1, 0:384]).astype(bf16)
    spare = pool[:, 0:SPARE, :].reshape(384, pool.shape[2])
    moved = jnp.dot(pick, spare, preferred_element_type=f32)
    kept = lax.broadcasted_iota(jnp.int32, moved.shape, 0) < have
    chosen = jnp.transpose(jnp.where(kept, target_ref[...].astype(f32), moved))
    chosen_ref[...] = chosen
    column = lax.broadcasted_iota(jnp.int32, (1, 384), 1)
    mask_pool = seq_pool = jnp.zeros((1, 384), f32)
    counts = []
    for k, place in enumerate(PLACES):
        mine = (column >= SPARE * k) & (column < SPARE * (k + 1))
        facts = pool[k, SPARE : SPARE + 16, :].astype(f32)
        mask_pool = jnp.where(mine, facts[0:1, 0:384], mask_pool)
        seq_pool = jnp.where(mine, (group_at(*place) // 2).astype(f32), seq_pool)
        counts.append(facts[1:2, 0:HALF])
    none = jnp.zeros((6, 384), f32)
    traits = lax.dot_general(
        jnp.concatenate([mask_pool, seq_pool, none], axis=0).astype(bf16), pick, (((1,), (1,)), ((), ())), preferred_element_type=f32
    )
    lane = lax.broadcasted_iota(jnp.int32, (1, HALF), 1)
    masked = (mask_ref[...] == 1).astype(f32)
    valid = jnp.where(lane < have, masked, traits[0:1])
    valid = jnp.where(lane < ROWS, valid, 0.0)
    sequence = jnp.where(lane < have, lax.axis_index("x").astype(f32), traits[1:2])
    nothing = jnp.zeros((1, HALF), f32)
    side_ref[...] = jnp.concatenate(
        [scale_ref[0:1], valid, sequence, sum(counts), counts[0] + counts[1]] + [nothing] * 3, axis=0
    )

    top_t = jnp.max(chosen, axis=0, keepdims=True)
    pow_t = jnp.exp(chosen - top_t)
    sum_t = jnp.sum(pow_t, axis=0, keepdims=True)
    dot_t = jnp.sum(pow_t * chosen, axis=0, keepdims=True)
    logits = logit_ref[...]
    top_d = jnp.max(logits, axis=0, keepdims=True)
    pow_d = jnp.exp(logits - top_d)
    stat_ref[...] = jnp.concatenate(
        [
            top_t,
            sum_t,
            dot_t,
            jnp.sum(pow_t * logits, axis=0, keepdims=True),
            top_d,
            jnp.sum(pow_d, axis=0, keepdims=True),
            jnp.sum(pow_d * logits, axis=0, keepdims=True),
            nothing,
        ],
        axis=0,
    )


def row_stats(lengths, logits, scales, target, loss_mask, slots, spares):
    vocab = logits.shape[0]
    return pl.pallas_call(
        stat_kernel,
        in_specs=[SCALARS] + [VECTORS] * 5 + [FAR] * 4,
        out_specs=[VECTORS] * 3,
        out_shape=(
            jax.ShapeDtypeStruct((vocab, HALF), f32),
            jax.ShapeDtypeStruct((8, HALF), f32),
            jax.ShapeDtypeStruct((8, HALF), f32),
        ),
        scratch_shapes=[
            pltpu.VMEM((GROUPS, SPARE + 16, vocab), bf16),
            pltpu.SemaphoreType.DMA((GROUPS,)),
        ],
        compiler_params=pltpu.CompilerParams(vmem_limit_bytes=16 * MIB),
        name="row_stats",
    )(lengths, logits, scales, target, loss_mask, slots, *spares)


def back_kernel(
    every_ref, logit_ref, chosen_ref, side_ref, gain_ref, united_ref, head_ref,
    mine_ref, other_ref,
):
    width = gain_ref.shape[1]
    every = every_ref[...]
    max_t = jnp.max(every[:, 0:1], axis=0)
    scale_t = jnp.exp(every[:, 0:1] - max_t[None])
    sum_t = jnp.sum(every[:, 1:2] * scale_t, axis=0)
    mean_tt = jnp.sum(every[:, 2:3] * scale_t, axis=0) / sum_t
    mean_tl = jnp.sum(every[:, 3:4] * scale_t, axis=0) / sum_t
    max_d = jnp.max(every[:, 4:5], axis=0)
    scale_d = jnp.exp(every[:, 4:5] - max_d[None])
    sum_d = jnp.sum(every[:, 5:6] * scale_d, axis=0)
    mean_dl = jnp.sum(every[:, 6:7] * scale_d, axis=0) / sum_d
    log_t = max_t + jnp.log(sum_t)
    log_d = max_d + jnp.log(sum_d)
    row_scale, valid, sequence = side_ref[0:1], side_ref[1:2], side_ref[2:3]
    kl = (mean_tt - mean_tl - log_t + log_d) * valid
    row = lax.broadcasted_iota(jnp.int32, (8, HALF), 0)
    sums = jnp.sum(jnp.where(row.astype(f32) == sequence, kl, 0.0), axis=1, keepdims=True)
    sums = jnp.broadcast_to(sums, (8, HALF))
    high = sums.astype(bf16).astype(f32)
    middle = (sums - high).astype(bf16).astype(f32)
    column = lax.broadcasted_iota(jnp.int32, (8, HALF), 1)
    third = jnp.where(column < 96, sums - high - middle, 0.0)
    sums = jnp.where(column < 32, high, jnp.where(column < 64, middle, third))

    weight = valid * row_scale
    grad = weight * (jnp.exp(logit_ref[...] - log_d) - jnp.exp(chosen_ref[...] - log_t))
    grad = jnp.transpose(grad)[0:ROWS].astype(bf16)
    lane = lax.broadcasted_iota(jnp.int32, (1, HALF), 1)
    share = ROWS // 16
    index = lax.axis_index(("z", "yl", "c"))
    mine = (lane >= index * share) & (lane < (index + 1) * share)
    cubic = jnp.where(mine, weight * row_scale * (mean_dl - mean_tl) / width, 0.0)
    cubic = jnp.transpose(jnp.broadcast_to(cubic, (HALF, HALF)))[0:ROWS, 0:1]
    for g in range(GROUPS):
        part = slice(g * 1024, (g + 1) * 1024)
        block = jnp.dot(grad, head_ref[:, part], preferred_element_type=f32)
        block = block * gain_ref[:, part] - cubic * united_ref[:, part].astype(f32)
        split_by_core(
            block, lax.axis_index("c") == 0, mine_ref.at[g], other_ref.at[g], sums
        )


def head_backward(every, logits, chosen, side, gain, united, head):
    return pl.pallas_call(
        back_kernel,
        in_specs=[VECTORS] * 7,
        out_specs=[VECTORS] * 2,
        out_shape=(
            jax.ShapeDtypeStruct((GROUPS, 8, PIECE + 8, 128), bf16),
            jax.ShapeDtypeStruct((GROUPS, 8, PIECE + 8, 128), bf16),
        ),
        compiler_params=pltpu.CompilerParams(vmem_limit_bytes=24 * MIB),
        name="head_backward",
    )(every, logits, chosen, side, gain, united, head)


def grad_kernel(side_ref, own_ref, other_ref, rows_ref, out_ref, wide, grads):
    @pl.when((pl.program_id(0) == 0) & (pl.program_id(1) == 0))
    def _():
        first = lax.axis_index("c") == 0
        for k, place in enumerate(PLACES):
            group = group_at(*place)
            for j in range(8):
                a = own_ref[j, group].astype(f32)
                b = other_ref[j, group].astype(f32)
                base = k * ROWS
                wide[base : base + PIECE, j * 128 : (j + 1) * 128] = jnp.where(first, a, b)
                wide[base + PIECE : base + ROWS, j * 128 : (j + 1) * 128] = jnp.where(first, b, a)
        grads[...] = wide[...].astype(bf16)

    factor = (2 * HALF) / jnp.maximum(side_ref[3:4, 0:1], 1.0)
    out_ref[0] = factor * lax.dot_general(
        rows_ref[0], grads[...], (((0,), (0,)), ((), ())), preferred_element_type=f32
    )


def weight_gradient(side, own, other, rows):
    total = GROUPS * ROWS
    whole = lambda shape: pl.BlockSpec(shape, lambda s, i: (0,) * len(shape))
    return pl.pallas_call(
        grad_kernel,
        grid=(3, 2),
        in_specs=[
            whole((8, HALF)),
            whole((8, GROUPS, PIECE, 128)),
            whole((8, GROUPS, PIECE, 128)),
            pl.BlockSpec((1, total, 256), lambda s, i: (s, 0, i)),
        ],
        out_specs=pl.BlockSpec((1, 256, 1024), lambda s, i: (s, i, 0)),
        out_shape=jax.ShapeDtypeStruct((3, 512, 1024), f32),
        scratch_shapes=[pltpu.VMEM((total, 1024), f32), pltpu.VMEM((total, 1024), bf16)],
        compiler_params=pltpu.CompilerParams(vmem_limit_bytes=40 * MIB),
        name="weight_gradient",
    )(side, own, other, rows)


def sum_kernel(piece_ref, out_ref, extra_ref):
    extra = jnp.zeros((8, 128), f32)
    for g in range(GROUPS):
        total = jnp.zeros((PIECE, 128), f32)
        for j in range(8):
            total = total + piece_ref[g * 8 + j, 0:PIECE, :].astype(f32)
        for k in range(8):
            out_ref[k, g] = total.astype(bf16)
        if piece_ref.shape[1] > PIECE:
            extra = extra + piece_ref[g * 8].astype(f32)[PIECE : PIECE + 8]
    extra_ref[...] = extra


def gather_sum(mine, other):
    pair = (mine.astype(f32) + swap(other, "c", 1, 2).astype(f32)).astype(bf16)
    received = lax.all_to_all(pair.reshape((64,) + pair.shape[2:]), CHIPS, 0, 0, tiled=True)
    copies, extra = pl.pallas_call(
        sum_kernel,
        in_specs=[VECTORS],
        out_specs=[VECTORS] * 2,
        out_shape=(
            jax.ShapeDtypeStruct((8, GROUPS, PIECE, 128), bf16),
            jax.ShapeDtypeStruct((8, 128), f32),
        ),
        compiler_params=pltpu.CompilerParams(vmem_limit_bytes=8 * MIB),
        name="sum_pieces",
    )(received)
    return copies, extra


def route(value, dx, dy):
    pairs = [(p * 2 + q, (p + dx) % 4 * 2 + (q ^ dy)) for p in range(4) for q in range(2)]
    return lax.ppermute(value, GROUP, pairs)


def local(captured, target_logits, unite_weight, norm_gain, head_weight, lengths, loss_mask):
    width = norm_gain.shape[0]
    own = captured.reshape(3, HALF, 512)
    target = target_logits.reshape(HALF, -1)
    far = route(own, 2, 0)
    over = route(own, 0, 1)
    right = route(own, 3, 0)
    left = route(own, 1, 0)
    far, near_target, later = lax.optimization_barrier((far, target, lengths))
    over_far = route(far, 0, 1)
    over_right = route(over, 3, 0)
    over_left = route(over, 1, 0)
    spare = spare_facts(lengths, loss_mask, near_target)
    pair = jnp.stack([spare, route(spare, 0, 1)])
    left, right, weight = lax.optimization_barrier((left, right, unite_weight))
    weight, near = stage(weight, own)
    wide_length = jnp.broadcast_to(later.astype(f32), (8, HALF))
    all_lengths = [wide_length] + [route(wide_length, dx, 0) for dx in range(1, 4)]
    over_far, pair = lax.optimization_barrier((over_far, pair))
    blocks = [near, over, left, right, far, over_left, over_right, over_far]
    rows, mine, other, slots = unite(blocks, all_lengths, weight)

    copies, _ = gather_sum(mine, other)
    copies, pair = lax.optimization_barrier((copies, pair))
    spares = [pair] + [route(pair, dx, 0) for dx in range(1, 4)]
    own_united = lax.all_to_all(copies, RING, 0, 0, tiled=True)
    own_united, spares[1], spares[3] = lax.optimization_barrier(
        (own_united, spares[1], spares[3])
    )
    other_united = swap(own_united, "c", 1, 2)
    gain = norm_gain.reshape(1, width)
    logits, scales, united, held = head_forward(own_united, other_united, gain, head_weight)
    chosen, stats, side = row_stats(
        lengths, logits, scales, target, loss_mask, slots, spares
    )
    every = spread(stats, ("z", "yl", "c"), 16)
    mine, other = head_backward(every, logits, chosen, side, gain, united, held)
    copies, sums = gather_sum(mine, other)
    own_grad = lax.all_to_all(copies, RING, 0, 0, tiled=True)
    seq_sum = jnp.sum(
        jnp.where(lax.iota(jnp.int32, GROUPS)[:, None] == lax.axis_index("x"), sums, 0.0)
    )
    seq_kl = (seq_sum / 32.0 / jnp.maximum(side[4, 0], 1.0)).reshape(1)
    own_grad, seq_kl = lax.optimization_barrier((own_grad, seq_kl))
    other_grad = swap(own_grad, "c", 1, 2)
    unite_grad = weight_gradient(side, own_grad, other_grad, rows)
    return (seq_kl, unite_grad)


def solution(mesh):
    fine = Mesh(mesh.devices.reshape(4, 2, 4, 2, 2), ALL)
    tensor = ("z", "yl", "c")
    placed = (
        P(None, "x", "yh", tensor),
        P("x", "yh", tensor),
        P(None, tensor, GROUP),
        P(),
        P(tensor, None),
        P("x"),
        P("x", "yh"),
    )
    return jax.shard_map(
        local,
        mesh=fine,
        in_specs=placed,
        out_specs=(P("x"), P(None, tensor, GROUP)),
        check_vma=False,
    )
```

```python
import functools

import jax
import jax.numpy as jnp
from jax import lax
from jax.experimental import pallas as pl
from jax.experimental.pallas import tpu as pltpu
from jax.sharding import Mesh, PartitionSpec as P

NORM_EPS = 1e-05
GROUP = ("x", "yh")
RING = ("z", "yl")
CHIPS = ("x", "yh", "z", "yl")
ALL = CHIPS + ("c",)
PLACES = [(0, 0), (0, 1), (3, 0), (1, 0), (2, 0), (3, 1), (1, 1), (2, 1)]
GROUPS = 8
HALF = 128
ROWS = 80
SPARE = HALF - ROWS
PIECE = ROWS // 2
MIB = 1 << 20
f32, bf16 = jnp.float32, jnp.bfloat16
SCALARS = pl.BlockSpec(memory_space=pltpu.SMEM)
VECTORS = pl.BlockSpec(memory_space=pltpu.VMEM)
FAR = pl.BlockSpec(memory_space=pltpu.HBM)


def group_at(dx, dy):
    return lax.rem(lax.axis_index("x") + dx, 4) * 2 + lax.rem(lax.axis_index("yh") + dy, 2)


def have_here(length):
    return jnp.clip(length - lax.axis_index("yh") * HALF, 0, HALF)


def spread(value, axes, count):
    return lax.all_to_all(
        jnp.broadcast_to(value[None], (count,) + value.shape), axes, 0, 0, tiled=True
    )


def swap(value, axis, bit, count):
    return lax.ppermute(value, axis, [(i, i ^ bit) for i in range(count)])


def spare_kernel(length_ref, mask_ref, target_ref, spare_ref):
    vocab = target_ref.shape[1]
    masked = (mask_ref[...] == 1).astype(f32)
    near = lax.broadcasted_iota(jnp.int32, (1, HALF), 1) < have_here(length_ref[0])
    count = jnp.sum(jnp.where(near, masked, 0.0), axis=1, keepdims=True)
    place = lax.broadcasted_iota(jnp.int32, (HALF, vocab), 0) - ROWS
    column = lax.broadcasted_iota(jnp.int32, (HALF, vocab), 1)
    tiled = jnp.zeros((HALF, vocab), f32)
    for k in range(GROUPS):
        tiled = jnp.where((column - SPARE * k == place) & (place >= 0), 1.0, tiled)
    repeated = jnp.dot(
        jnp.broadcast_to(masked, (8, HALF)).astype(bf16),
        tiled.astype(bf16),
        preferred_element_type=f32,
    )[0:1]
    row = lax.broadcasted_iota(jnp.int32, (16, vocab), 0)
    facts = jnp.where(row == 0, repeated, jnp.where(row == 1, count, 0.0))
    spare_ref[0:SPARE, :] = target_ref[ROWS:HALF, :]
    spare_ref[SPARE : SPARE + 16, :] = facts.astype(bf16)


def spare_facts(lengths, loss_mask, target):
    return pl.pallas_call(
        spare_kernel,
        in_specs=[SCALARS, VECTORS, VECTORS],
        out_specs=VECTORS,
        out_shape=jax.ShapeDtypeStruct((SPARE + 16, target.shape[1]), bf16),
        compiler_params=pltpu.CompilerParams(vmem_limit_bytes=8 * MIB),
        name="spare_facts",
    )(lengths, loss_mask, target)


def stage_kernel(hbm_weight, hbm_cap, weight_ref, cap_ref, sems):
    copies = [
        pltpu.make_async_copy(hbm_weight, weight_ref, sems.at[0]),
        pltpu.make_async_copy(hbm_cap, cap_ref, sems.at[1]),
    ]
    for copy in copies:
        copy.start()
    for copy in copies:
        copy.wait()


def stage(weight, captured):
    return pl.pallas_call(
        stage_kernel,
        in_specs=[FAR, FAR],
        out_specs=[VECTORS] * 2,
        out_shape=(
            jax.ShapeDtypeStruct(weight.shape, bf16),
            jax.ShapeDtypeStruct(captured.shape, bf16),
        ),
        scratch_shapes=[pltpu.SemaphoreType.DMA((2,))],
        compiler_params=pltpu.CompilerParams(vmem_limit_bytes=8 * MIB),
        name="stage",
    )(weight, captured)


def split_by_core(block, first, mine_ref, other_ref, extra=None):
    for j in range(8):
        upper = block[0:PIECE, j * 128 : (j + 1) * 128]
        lower = block[PIECE:ROWS, j * 128 : (j + 1) * 128]
        mine = jnp.where(first, upper, lower)
        other = jnp.where(first, lower, upper)
        if extra is not None:
            mine = jnp.concatenate([mine, extra], axis=0)
            other = jnp.concatenate([other, jnp.zeros_like(extra)], axis=0)
        mine_ref[j] = mine.astype(bf16)
        other_ref[j] = other.astype(bf16)


def unite_kernel(*refs):
    blocks, length_refs = refs[:GROUPS], refs[GROUPS : GROUPS + 3]
    weight_ref, near_rows_ref, far_rows_ref, mine_ref, other_ref, slot_ref = refs[GROUPS + 3 :]
    lengths = [jnp.broadcast_to(ref[0:1, 0:1], (1, 512)) for ref in length_refs]
    lengths = {0: lengths[0], 3: lengths[1], 1: lengths[2], 2: GROUPS * ROWS - sum(lengths)}
    first = lax.axis_index("c") == 0
    groups = [group_at(*place) for place in PLACES]
    lane = lax.broadcasted_iota(jnp.int32, (1, 512), 1).astype(f32)
    have = [
        jnp.clip(
            lengths[dx]
            - lax.rem(lax.axis_index("yh") + dy, 2).astype(f32) * HALF,
            0.0,
            float(HALF),
        )
        for dx, dy in PLACES
    ]
    more = [jnp.maximum(h - ROWS, 0.0) for h in have]
    less = [jnp.maximum(ROWS - h, 0.0) for h in have]

    def before(amounts, k):
        total = jnp.zeros((1, 512), f32)
        for m in range(GROUPS):
            if m != k:
                total = total + amounts[m] * (groups[m] < groups[k]).astype(f32)
        return total

    order = jnp.full((1, 512), -1.0, f32)
    for k in range(GROUPS):
        place = lane - SPARE * k
        mine = (place >= 0) & (place < SPARE)
        order = jnp.where(mine & (place < have[k] - ROWS), before(more, k) + place, order)
    slot = jnp.full((1, 512), -1.0, f32)
    for k in range(GROUPS):
        offset = order - before(less, k)
        mine = (order >= 0) & (offset >= 0) & (offset < ROWS - have[k])
        slot = jnp.where(mine, ROWS * k + have[k] + offset, slot)
    slot_ref[...] = jnp.broadcast_to(slot, (8, 512))
    for half in range(2):
        row = lax.broadcasted_iota(jnp.int32, (4 * ROWS, 384), 0) + half * 4 * ROWS
        pick = (row.astype(f32) == slot[:, :384]).astype(bf16)
        total = None
        for s in range(3):
            pool = jnp.concatenate([block[s, ROWS:HALF, :] for block in blocks], axis=0)
            moved = jnp.dot(pick, pool, preferred_element_type=f32)
            kept = []
            for k in range(4 * half, 4 * half + 4):
                own = blocks[k][s, 0:ROWS, :].astype(f32)
                within = lax.broadcasted_iota(jnp.int32, (ROWS, 512), 0).astype(f32) < have[k]
                base = (k - 4 * half) * ROWS
                kept.append(jnp.where(within, own, moved[base : base + ROWS]))
            upper = jnp.concatenate([rows[0:PIECE] for rows in kept], axis=0)
            lower = jnp.concatenate([rows[PIECE:ROWS] for rows in kept], axis=0)
            part = pl.ds(half * 4 * PIECE, 4 * PIECE)
            near_rows_ref[s, part, :] = jnp.where(first, upper, lower).astype(bf16)
            far_rows_ref[s, part, :] = jnp.where(first, lower, upper).astype(bf16)
            rows = jnp.concatenate(kept, axis=0).astype(bf16)
            term = jnp.dot(rows, weight_ref[s], preferred_element_type=f32)
            total = term if total is None else total + term
        for k in range(4):
            group = groups[4 * half + k]
            split_by_core(
                total[k * ROWS : (k + 1) * ROWS], first, mine_ref.at[group], other_ref.at[group]
            )


def unite(blocks, lengths, weight):
    return pl.pallas_call(
        unite_kernel,
        in_specs=[VECTORS] * (GROUPS + 4),
        out_specs=[VECTORS] * 5,
        out_shape=(
            jax.ShapeDtypeStruct((3, GROUPS * PIECE, 512), bf16),
            jax.ShapeDtypeStruct((3, GROUPS * PIECE, 512), bf16),
            jax.ShapeDtypeStruct((GROUPS, 8, PIECE, 128), bf16),
            jax.ShapeDtypeStruct((GROUPS, 8, PIECE, 128), bf16),
            jax.ShapeDtypeStruct((8, 512), f32),
        ),
        compiler_params=pltpu.CompilerParams(vmem_limit_bytes=24 * MIB),
        name="unite",
    )(*blocks, *lengths, weight)


def head_kernel(
    own_ref, other_ref, gain_ref, head_ref,
    logit_ref, scale_ref, united_ref, held, wide, normed, sems,
):
    width = wide.shape[1]
    tile = head_ref.shape[0] // 8
    loads = [
        pltpu.make_async_copy(
            head_ref.at[pl.ds(i * tile, tile)], held.at[pl.ds(i * tile, tile)], sems.at[i]
        )
        for i in range(8)
    ]
    for copy in loads[:3]:
        copy.start()

    first = lax.axis_index("c") == 0
    wide[ROWS:HALF, :] = jnp.zeros((HALF - ROWS, width), f32)
    for g in range(GROUPS):
        for j in range(8):
            column = (g * 8 + j) * 128
            a = own_ref[j, g].astype(f32)
            b = other_ref[j, g].astype(f32)
            wide[0:PIECE, column : column + 128] = jnp.where(first, a, b)
            wide[PIECE:ROWS, column : column + 128] = jnp.where(first, b, a)
    square = jnp.zeros((HALF, 1), f32)
    for g in range(GROUPS):
        values = wide[:, g * 1024 : (g + 1) * 1024]
        square = square + jnp.sum(values * values, axis=1, keepdims=True)
    scale = lax.rsqrt(square / width + NORM_EPS)
    for g in range(GROUPS):
        part = slice(g * 1024, (g + 1) * 1024)
        values = wide[:, part]
        united_ref[:, part] = values[0:ROWS].astype(bf16)
        normed[part, :] = jnp.transpose(values * scale * gain_ref[:, part]).astype(bf16)

    scale_ref[...] = jnp.transpose(jnp.broadcast_to(scale, (HALF, HALF)))[0:8]
    for i in range(0, 8, 2):
        for k in (i, i + 1):
            loads[k].wait()
            if k + 3 < 8:
                loads[k + 3].start()
        part = slice(i * tile, (i + 2) * tile)
        logit_ref[part, :] = jnp.dot(held[part, :], normed[...], preferred_element_type=f32)


def head_forward(own, other, gain, head):
    vocab, width = head.shape
    return pl.pallas_call(
        head_kernel,
        in_specs=[VECTORS] * 3 + [FAR],
        out_specs=[VECTORS] * 4,
        out_shape=(
            jax.ShapeDtypeStruct((vocab, HALF), f32),
            jax.ShapeDtypeStruct((8, HALF), f32),
            jax.ShapeDtypeStruct((ROWS, width), bf16),
            jax.ShapeDtypeStruct((vocab, width), bf16),
        ),
        scratch_shapes=[
            pltpu.VMEM((HALF, width), f32),
            pltpu.VMEM((width, HALF), bf16),
            pltpu.SemaphoreType.DMA((8,)),
        ],
        compiler_params=pltpu.CompilerParams(vmem_limit_bytes=24 * MIB),
        cost_estimate=pl.CostEstimate(
            flops=4 * HALF * vocab * width, bytes_accessed=2 * vocab * width, transcendentals=0
        ),
        name="head_forward",
    )(own, other, gain, head)


def stat_kernel(
    length_ref, logit_ref, scale_ref, target_ref, mask_ref, slot_ref, *refs
):
    spares = refs[:4]
    chosen_ref, stat_ref, side_ref, pool, pool_sems = refs[4:]
    moves = [
        pltpu.make_async_copy(spares[-dx % 4].at[dy], pool.at[k], pool_sems.at[k])
        for k, (dx, dy) in enumerate(PLACES)
    ]
    for copy in moves:
        copy.start()
    for copy in moves:
        copy.wait()
    have = have_here(length_ref[0])
    row = lax.broadcasted_iota(jnp.int32, (HALF, 384), 0)
    pick = (row.astype(f32) == slot_ref[0:1, 0:384]).astype(bf16)
    spare = pool[:, 0:SPARE, :].reshape(384, pool.shape[2])
    moved = jnp.dot(pick, spare, preferred_element_type=f32)
    kept = lax.broadcasted_iota(jnp.int32, moved.shape, 0) < have
    chosen = jnp.transpose(jnp.where(kept, target_ref[...].astype(f32), moved))
    chosen_ref[...] = chosen
    column = lax.broadcasted_iota(jnp.int32, (1, 384), 1)
    mask_pool = seq_pool = jnp.zeros((1, 384), f32)
    counts = []
    for k, place in enumerate(PLACES):
        mine = (column >= SPARE * k) & (column < SPARE * (k + 1))
        facts = pool[k, SPARE : SPARE + 16, :].astype(f32)
        mask_pool = jnp.where(mine, facts[0:1, 0:384], mask_pool)
        seq_pool = jnp.where(mine, (group_at(*place) // 2).astype(f32), seq_pool)
        counts.append(facts[1:2, 0:HALF])
    none = jnp.zeros((6, 384), f32)
    traits = lax.dot_general(
        jnp.concatenate([mask_pool, seq_pool, none], axis=0).astype(bf16), pick, (((1,), (1,)), ((), ())), preferred_element_type=f32
    )
    lane = lax.broadcasted_iota(jnp.int32, (1, HALF), 1)
    masked = (mask_ref[...] == 1).astype(f32)
    valid = jnp.where(lane < have, masked, traits[0:1])
    valid = jnp.where(lane < ROWS, valid, 0.0)
    sequence = jnp.where(lane < have, lax.axis_index("x").astype(f32), traits[1:2])
    nothing = jnp.zeros((1, HALF), f32)
    side_ref[...] = jnp.concatenate(
        [scale_ref[0:1], valid, sequence, sum(counts), counts[0] + counts[1]] + [nothing] * 3, axis=0
    )

    top_t = jnp.max(chosen, axis=0, keepdims=True)
    pow_t = jnp.exp(chosen - top_t)
    sum_t = jnp.sum(pow_t, axis=0, keepdims=True)
    dot_t = jnp.sum(pow_t * chosen, axis=0, keepdims=True)
    logits = logit_ref[...]
    top_d = jnp.max(logits, axis=0, keepdims=True)
    pow_d = jnp.exp(logits - top_d)
    stat_ref[...] = jnp.concatenate(
        [
            top_t,
            sum_t,
            dot_t,
            jnp.sum(pow_t * logits, axis=0, keepdims=True),
            top_d,
            jnp.sum(pow_d, axis=0, keepdims=True),
            jnp.sum(pow_d * logits, axis=0, keepdims=True),
            nothing,
        ],
        axis=0,
    )


def row_stats(lengths, logits, scales, target, loss_mask, slots, spares):
    vocab = logits.shape[0]
    return pl.pallas_call(
        stat_kernel,
        in_specs=[SCALARS] + [VECTORS] * 5 + [FAR] * 4,
        out_specs=[VECTORS] * 3,
        out_shape=(
            jax.ShapeDtypeStruct((vocab, HALF), f32),
            jax.ShapeDtypeStruct((8, HALF), f32),
            jax.ShapeDtypeStruct((8, HALF), f32),
        ),
        scratch_shapes=[
            pltpu.VMEM((GROUPS, SPARE + 16, vocab), bf16),
            pltpu.SemaphoreType.DMA((GROUPS,)),
        ],
        compiler_params=pltpu.CompilerParams(vmem_limit_bytes=16 * MIB),
        name="row_stats",
    )(lengths, logits, scales, target, loss_mask, slots, *spares)


def back_kernel(
    every_ref, logit_ref, chosen_ref, side_ref, gain_ref, united_ref, head_ref,
    mine_ref, other_ref,
):
    width = gain_ref.shape[1]
    every = every_ref[...]
    max_t = jnp.max(every[:, 0:1], axis=0)
    scale_t = jnp.exp(every[:, 0:1] - max_t[None])
    sum_t = jnp.sum(every[:, 1:2] * scale_t, axis=0)
    mean_tt = jnp.sum(every[:, 2:3] * scale_t, axis=0) / sum_t
    mean_tl = jnp.sum(every[:, 3:4] * scale_t, axis=0) / sum_t
    max_d = jnp.max(every[:, 4:5], axis=0)
    scale_d = jnp.exp(every[:, 4:5] - max_d[None])
    sum_d = jnp.sum(every[:, 5:6] * scale_d, axis=0)
    mean_dl = jnp.sum(every[:, 6:7] * scale_d, axis=0) / sum_d
    log_t = max_t + jnp.log(sum_t)
    log_d = max_d + jnp.log(sum_d)
    row_scale, valid, sequence = side_ref[0:1], side_ref[1:2], side_ref[2:3]
    kl = (mean_tt - mean_tl - log_t + log_d) * valid
    row = lax.broadcasted_iota(jnp.int32, (8, HALF), 0)
    sums = jnp.sum(jnp.where(row.astype(f32) == sequence, kl, 0.0), axis=1, keepdims=True)
    sums = jnp.broadcast_to(sums, (8, HALF))
    high = sums.astype(bf16).astype(f32)
    middle = (sums - high).astype(bf16).astype(f32)
    column = lax.broadcasted_iota(jnp.int32, (8, HALF), 1)
    third = jnp.where(column < 96, sums - high - middle, 0.0)
    sums = jnp.where(column < 32, high, jnp.where(column < 64, middle, third))

    weight = valid * row_scale
    grad = weight * (jnp.exp(logit_ref[...] - log_d) - jnp.exp(chosen_ref[...] - log_t))
    grad = jnp.transpose(grad)[0:ROWS].astype(bf16)
    lane = lax.broadcasted_iota(jnp.int32, (1, HALF), 1)
    share = ROWS // 16
    index = lax.axis_index(("z", "yl", "c"))
    mine = (lane >= index * share) & (lane < (index + 1) * share)
    cubic = jnp.where(mine, weight * row_scale * (mean_dl - mean_tl) / width, 0.0)
    cubic = jnp.transpose(jnp.broadcast_to(cubic, (HALF, HALF)))[0:ROWS, 0:1]
    for g in range(GROUPS):
        part = slice(g * 1024, (g + 1) * 1024)
        block = jnp.dot(grad, head_ref[:, part], preferred_element_type=f32)
        block = block * gain_ref[:, part] - cubic * united_ref[:, part].astype(f32)
        split_by_core(
            block, lax.axis_index("c") == 0, mine_ref.at[g], other_ref.at[g], sums
        )


def head_backward(every, logits, chosen, side, gain, united, head):
    return pl.pallas_call(
        back_kernel,
        in_specs=[VECTORS] * 7,
        out_specs=[VECTORS] * 2,
        out_shape=(
            jax.ShapeDtypeStruct((GROUPS, 8, PIECE + 8, 128), bf16),
            jax.ShapeDtypeStruct((GROUPS, 8, PIECE + 8, 128), bf16),
        ),
        compiler_params=pltpu.CompilerParams(vmem_limit_bytes=24 * MIB),
        name="head_backward",
    )(every, logits, chosen, side, gain, united, head)


def assemble(grad_ref, wide, grads):
    for k, place in enumerate(PLACES):
        group = group_at(*place)
        for j in range(8):
            wide[k * PIECE : (k + 1) * PIECE, j * 128 : (j + 1) * 128] = grad_ref[
                j, group
            ].astype(f32)
    grads[...] = wide[...].astype(bf16)


def near_kernel(grad_ref, rows_ref, out_ref, wide, grads):
    assemble(grad_ref, wide, grads)
    for s in range(3):
        out_ref[s] = lax.dot_general(
            rows_ref[s], grads[...], (((0,), (0,)), ((), ())), preferred_element_type=f32
        )


def far_kernel(side_ref, grad_ref, rows_ref, near_ref, out_ref, wide, grads):
    @pl.when((pl.program_id(0) == 0) & (pl.program_id(1) == 0))
    def _():
        assemble(grad_ref, wide, grads)

    factor = (2 * HALF) / jnp.maximum(side_ref[3:4, 0:1], 1.0)
    here = near_ref[pl.program_id(0), pl.ds(pl.program_id(1) * 256, 256), :]
    out_ref[0] = factor * (
        here
        + lax.dot_general(
            rows_ref[0], grads[...], (((0,), (0,)), ((), ())), preferred_element_type=f32
        )
    )


def near_gradient(own, rows):
    total = GROUPS * PIECE
    return pl.pallas_call(
        near_kernel,
        in_specs=[VECTORS] * 2,
        out_specs=VECTORS,
        out_shape=jax.ShapeDtypeStruct((3, 512, 1024), f32),
        scratch_shapes=[pltpu.VMEM((total, 1024), f32), pltpu.VMEM((total, 1024), bf16)],
        compiler_params=pltpu.CompilerParams(vmem_limit_bytes=16 * MIB),
        cost_estimate=pl.CostEstimate(
            flops=6 * total * 512 * 1024, bytes_accessed=6 * MIB, transcendentals=0
        ),
        name="near_gradient",
    )(own, rows)


def weight_gradient(side, other, rows, near):
    total = GROUPS * PIECE
    whole = lambda shape: pl.BlockSpec(shape, lambda s, i: (0,) * len(shape))
    return pl.pallas_call(
        far_kernel,
        grid=(3, 2),
        in_specs=[
            whole((8, HALF)),
            whole((8, GROUPS, PIECE, 128)),
            pl.BlockSpec((1, total, 256), lambda s, i: (s, 0, i)),
            VECTORS,
        ],
        out_specs=pl.BlockSpec((1, 256, 1024), lambda s, i: (s, i, 0)),
        out_shape=jax.ShapeDtypeStruct((3, 512, 1024), f32),
        scratch_shapes=[pltpu.VMEM((total, 1024), f32), pltpu.VMEM((total, 1024), bf16)],
        compiler_params=pltpu.CompilerParams(vmem_limit_bytes=24 * MIB),
        name="weight_gradient",
    )(side, other, rows, near)


def sum_kernel(piece_ref, out_ref, extra_ref):
    extra = jnp.zeros((8, 128), f32)
    for g in range(GROUPS):
        total = jnp.zeros((PIECE, 128), f32)
        for j in range(8):
            total = total + piece_ref[g * 8 + j, 0:PIECE, :].astype(f32)
        for k in range(8):
            out_ref[k, g] = total.astype(bf16)
        if piece_ref.shape[1] > PIECE:
            extra = extra + piece_ref[g * 8].astype(f32)[PIECE : PIECE + 8]
    extra_ref[...] = extra


def gather_sum(mine, other):
    pair = (mine.astype(f32) + swap(other, "c", 1, 2).astype(f32)).astype(bf16)
    received = lax.all_to_all(pair.reshape((64,) + pair.shape[2:]), CHIPS, 0, 0, tiled=True)
    copies, extra = pl.pallas_call(
        sum_kernel,
        in_specs=[VECTORS],
        out_specs=[VECTORS] * 2,
        out_shape=(
            jax.ShapeDtypeStruct((8, GROUPS, PIECE, 128), bf16),
            jax.ShapeDtypeStruct((8, 128), f32),
        ),
        compiler_params=pltpu.CompilerParams(vmem_limit_bytes=8 * MIB),
        name="sum_pieces",
    )(received)
    return copies, extra


def route(value, dx, dy):
    pairs = [(p * 2 + q, (p + dx) % 4 * 2 + (q ^ dy)) for p in range(4) for q in range(2)]
    return lax.ppermute(value, GROUP, pairs)


def local(captured, target_logits, unite_weight, norm_gain, head_weight, lengths, loss_mask):
    width = norm_gain.shape[0]
    own = captured.reshape(3, HALF, 512)
    target = target_logits.reshape(HALF, -1)
    far = route(own, 2, 0)
    over = route(own, 0, 1)
    right = route(own, 3, 0)
    left = route(own, 1, 0)
    far, near_target, later = lax.optimization_barrier((far, target, lengths))
    over_far = route(far, 0, 1)
    over_right = route(over, 3, 0)
    over_left = route(over, 1, 0)
    spare = spare_facts(lengths, loss_mask, near_target)
    pair = jnp.stack([spare, route(spare, 0, 1)])
    left, right, weight = lax.optimization_barrier((left, right, unite_weight))
    weight, near = stage(weight, own)
    wide_length = jnp.broadcast_to(later.astype(f32), (8, HALF))
    all_lengths = [wide_length, route(wide_length, 1, 0), route(wide_length, 3, 0)]
    over_far, pair = lax.optimization_barrier((over_far, pair))
    blocks = [near, over, left, right, far, over_left, over_right, over_far]
    near_rows, far_rows, mine, other, slots = unite(blocks, all_lengths, weight)

    copies, _ = gather_sum(mine, other)
    copies, pair = lax.optimization_barrier((copies, pair))
    spares = [pair] + [route(pair, dx, 0) for dx in range(1, 4)]
    own_united = lax.all_to_all(copies, RING, 0, 0, tiled=True)
    own_united, spares[1], spares[3] = lax.optimization_barrier(
        (own_united, spares[1], spares[3])
    )
    other_united = swap(own_united, "c", 1, 2)
    gain = norm_gain.reshape(1, width)
    logits, scales, united, held = head_forward(own_united, other_united, gain, head_weight)
    chosen, stats, side = row_stats(
        lengths, logits, scales, target, loss_mask, slots, spares
    )
    every = spread(stats, ("z", "yl", "c"), 16)
    mine, other = head_backward(every, logits, chosen, side, gain, united, held)
    copies, sums = gather_sum(mine, other)
    own_grad = lax.all_to_all(copies, RING, 0, 0, tiled=True)
    seq_sum = jnp.sum(
        jnp.where(lax.iota(jnp.int32, GROUPS)[:, None] == lax.axis_index("x"), sums, 0.0)
    )
    seq_kl = (seq_sum / 32.0 / jnp.maximum(side[4, 0], 1.0)).reshape(1)
    own_grad, seq_kl = lax.optimization_barrier((own_grad, seq_kl))
    other_grad = swap(own_grad, "c", 1, 2)
    near_part = near_gradient(own_grad, near_rows)
    unite_grad = weight_gradient(side, other_grad, far_rows, near_part)
    return (seq_kl, unite_grad)


def solution(mesh):
    fine = Mesh(mesh.devices.reshape(4, 2, 4, 2, 2), ALL)
    tensor = ("z", "yl", "c")
    placed = (
        P(None, "x", "yh", tensor),
        P("x", "yh", tensor),
        P(None, tensor, GROUP),
        P(),
        P(tensor, None),
        P("x"),
        P("x", "yh"),
    )
    return jax.shard_map(
        local,
        mesh=fine,
        in_specs=placed,
        out_specs=(P("x"), P(None, tensor, GROUP)),
        check_vma=False,
    )
```

```python
import functools

import jax
import jax.numpy as jnp
from jax import lax
from jax.experimental import pallas as pl
from jax.experimental.pallas import tpu as pltpu
from jax.sharding import Mesh, PartitionSpec as P

NORM_EPS = 1e-05
GROUP = ("x", "yh")
RING = ("z", "yl")
CHIPS = ("x", "yh", "z", "yl")
ALL = CHIPS + ("c",)
PLACES = [(0, 0), (0, 1), (3, 0), (1, 0), (2, 0), (3, 1), (1, 1), (2, 1)]
GROUPS = 8
HALF = 128
ROWS = 80
SPARE = HALF - ROWS
PIECE = ROWS // 2
MIB = 1 << 20
f32, bf16 = jnp.float32, jnp.bfloat16
SCALARS = pl.BlockSpec(memory_space=pltpu.SMEM)
VECTORS = pl.BlockSpec(memory_space=pltpu.VMEM)
FAR = pl.BlockSpec(memory_space=pltpu.HBM)


def group_at(dx, dy):
    return lax.rem(lax.axis_index("x") + dx, 4) * 2 + lax.rem(lax.axis_index("yh") + dy, 2)


def have_here(length):
    return jnp.clip(length - lax.axis_index("yh") * HALF, 0, HALF)


def spread(value, axes, count):
    return lax.all_to_all(
        jnp.broadcast_to(value[None], (count,) + value.shape), axes, 0, 0, tiled=True
    )


def swap(value, axis, bit, count):
    return lax.ppermute(value, axis, [(i, i ^ bit) for i in range(count)])


def spare_kernel(length_ref, mask_ref, target_ref, spare_ref):
    vocab = target_ref.shape[1]
    masked = (mask_ref[...] == 1).astype(f32)
    near = lax.broadcasted_iota(jnp.int32, (1, HALF), 1) < have_here(length_ref[0])
    count = jnp.sum(jnp.where(near, masked, 0.0), axis=1, keepdims=True)
    place = lax.broadcasted_iota(jnp.int32, (HALF, vocab), 0) - ROWS
    column = lax.broadcasted_iota(jnp.int32, (HALF, vocab), 1)
    tiled = jnp.zeros((HALF, vocab), f32)
    for k in range(GROUPS):
        tiled = jnp.where((column - SPARE * k == place) & (place >= 0), 1.0, tiled)
    repeated = jnp.dot(
        jnp.broadcast_to(masked, (8, HALF)).astype(bf16),
        tiled.astype(bf16),
        preferred_element_type=f32,
    )[0:1]
    row = lax.broadcasted_iota(jnp.int32, (16, vocab), 0)
    facts = jnp.where(row == 0, repeated, jnp.where(row == 1, count, 0.0))
    spare_ref[0:SPARE, :] = target_ref[ROWS:HALF, :]
    spare_ref[SPARE : SPARE + 16, :] = facts.astype(bf16)


def spare_facts(lengths, loss_mask, target):
    return pl.pallas_call(
        spare_kernel,
        in_specs=[SCALARS, VECTORS, VECTORS],
        out_specs=VECTORS,
        out_shape=jax.ShapeDtypeStruct((SPARE + 16, target.shape[1]), bf16),
        compiler_params=pltpu.CompilerParams(vmem_limit_bytes=8 * MIB),
        name="spare_facts",
    )(lengths, loss_mask, target)


def stage_kernel(hbm_weight, hbm_cap, weight_ref, cap_ref, sems):
    copies = [
        pltpu.make_async_copy(hbm_weight, weight_ref, sems.at[0]),
        pltpu.make_async_copy(hbm_cap, cap_ref, sems.at[1]),
    ]
    for copy in copies:
        copy.start()
    for copy in copies:
        copy.wait()


def stage(weight, captured):
    return pl.pallas_call(
        stage_kernel,
        in_specs=[FAR, FAR],
        out_specs=[VECTORS] * 2,
        out_shape=(
            jax.ShapeDtypeStruct(weight.shape, bf16),
            jax.ShapeDtypeStruct(captured.shape, bf16),
        ),
        scratch_shapes=[pltpu.SemaphoreType.DMA((2,))],
        compiler_params=pltpu.CompilerParams(vmem_limit_bytes=8 * MIB),
        name="stage",
    )(weight, captured)


def split_by_core(block, first, mine_ref, other_ref, extra=None):
    for j in range(8):
        upper = block[0:PIECE, j * 128 : (j + 1) * 128]
        lower = block[PIECE:ROWS, j * 128 : (j + 1) * 128]
        mine = jnp.where(first, upper, lower)
        other = jnp.where(first, lower, upper)
        if extra is not None:
            mine = jnp.concatenate([mine, extra], axis=0)
            other = jnp.concatenate([other, jnp.zeros_like(extra)], axis=0)
        mine_ref[j] = mine.astype(bf16)
        other_ref[j] = other.astype(bf16)


def unite_kernel(*refs):
    blocks, length_refs = refs[:GROUPS], refs[GROUPS : GROUPS + 3]
    weight_ref, near_rows_ref, far_rows_ref, mine_ref, other_ref, slot_ref = refs[GROUPS + 3 :]
    lengths = [jnp.broadcast_to(ref[0:1, 0:1], (1, 512)) for ref in length_refs]
    lengths = {0: lengths[0], 3: lengths[1], 1: lengths[2], 2: GROUPS * ROWS - sum(lengths)}
    first = lax.axis_index("c") == 0
    groups = [group_at(*place) for place in PLACES]
    lane = lax.broadcasted_iota(jnp.int32, (1, 512), 1).astype(f32)
    have = [
        jnp.clip(
            lengths[dx]
            - lax.rem(lax.axis_index("yh") + dy, 2).astype(f32) * HALF,
            0.0,
            float(HALF),
        )
        for dx, dy in PLACES
    ]
    more = [jnp.maximum(h - ROWS, 0.0) for h in have]
    less = [jnp.maximum(ROWS - h, 0.0) for h in have]

    def before(amounts, k):
        total = jnp.zeros((1, 512), f32)
        for m in range(GROUPS):
            if m != k:
                total = total + amounts[m] * (groups[m] < groups[k]).astype(f32)
        return total

    order = jnp.full((1, 512), -1.0, f32)
    for k in range(GROUPS):
        place = lane - SPARE * k
        mine = (place >= 0) & (place < SPARE)
        order = jnp.where(mine & (place < have[k] - ROWS), before(more, k) + place, order)
    slot = jnp.full((1, 512), -1.0, f32)
    for k in range(GROUPS):
        offset = order - before(less, k)
        mine = (order >= 0) & (offset >= 0) & (offset < ROWS - have[k])
        slot = jnp.where(mine, ROWS * k + have[k] + offset, slot)
    slot_ref[...] = jnp.broadcast_to(slot, (8, 512))
    for half in range(2):
        row = lax.broadcasted_iota(jnp.int32, (4 * ROWS, 384), 0) + half * 4 * ROWS
        pick = (row.astype(f32) == slot[:, :384]).astype(bf16)
        total = None
        for s in range(3):
            pool = jnp.concatenate([block[s, ROWS:HALF, :] for block in blocks], axis=0)
            moved = jnp.dot(pick, pool, preferred_element_type=f32)
            kept = []
            for k in range(4 * half, 4 * half + 4):
                own = blocks[k][s, 0:ROWS, :].astype(f32)
                within = lax.broadcasted_iota(jnp.int32, (ROWS, 512), 0).astype(f32) < have[k]
                base = (k - 4 * half) * ROWS
                kept.append(jnp.where(within, own, moved[base : base + ROWS]))
            upper = jnp.concatenate([rows[0:PIECE] for rows in kept], axis=0)
            lower = jnp.concatenate([rows[PIECE:ROWS] for rows in kept], axis=0)
            part = pl.ds(half * 4 * PIECE, 4 * PIECE)
            near_rows_ref[s, part, :] = jnp.where(first, upper, lower).astype(bf16)
            far_rows_ref[s, part, :] = jnp.where(first, lower, upper).astype(bf16)
            rows = jnp.concatenate(kept, axis=0).astype(bf16)
            term = jnp.dot(rows, weight_ref[s], preferred_element_type=f32)
            total = term if total is None else total + term
        for k in range(4):
            group = groups[4 * half + k]
            split_by_core(
                total[k * ROWS : (k + 1) * ROWS], first, mine_ref.at[group], other_ref.at[group]
            )


def unite(blocks, lengths, weight):
    return pl.pallas_call(
        unite_kernel,
        in_specs=[VECTORS] * (GROUPS + 4),
        out_specs=[VECTORS] * 5,
        out_shape=(
            jax.ShapeDtypeStruct((3, GROUPS * PIECE, 512), bf16),
            jax.ShapeDtypeStruct((3, GROUPS * PIECE, 512), bf16),
            jax.ShapeDtypeStruct((GROUPS, 8, PIECE, 128), bf16),
            jax.ShapeDtypeStruct((GROUPS, 8, PIECE, 128), bf16),
            jax.ShapeDtypeStruct((8, 512), f32),
        ),
        compiler_params=pltpu.CompilerParams(vmem_limit_bytes=24 * MIB),
        name="unite",
    )(*blocks, *lengths, weight)


def head_kernel(
    own_ref, other_ref, gain_ref, head_ref,
    logit_ref, scale_ref, united_ref, held, wide, normed, sems,
):
    width = wide.shape[1]
    tile = head_ref.shape[0] // 8
    loads = [
        pltpu.make_async_copy(
            head_ref.at[pl.ds(i * tile, tile)], held.at[pl.ds(i * tile, tile)], sems.at[i]
        )
        for i in range(8)
    ]
    for copy in loads[:3]:
        copy.start()

    first = lax.axis_index("c") == 0
    wide[ROWS:HALF, :] = jnp.zeros((HALF - ROWS, width), f32)
    for g in range(GROUPS):
        for j in range(8):
            column = (g * 8 + j) * 128
            a = own_ref[j, g].astype(f32)
            b = other_ref[j, g].astype(f32)
            wide[0:PIECE, column : column + 128] = jnp.where(first, a, b)
            wide[PIECE:ROWS, column : column + 128] = jnp.where(first, b, a)
    square = jnp.zeros((HALF, 1), f32)
    for g in range(GROUPS):
        values = wide[:, g * 1024 : (g + 1) * 1024]
        square = square + jnp.sum(values * values, axis=1, keepdims=True)
    scale = lax.rsqrt(square / width + NORM_EPS)
    for g in range(GROUPS):
        part = slice(g * 1024, (g + 1) * 1024)
        values = wide[:, part]
        united_ref[:, part] = values[0:ROWS].astype(bf16)
        normed[part, :] = jnp.transpose(values * scale * gain_ref[:, part]).astype(bf16)

    scale_ref[...] = jnp.transpose(jnp.broadcast_to(scale, (HALF, HALF)))[0:8]
    for i in range(0, 8, 2):
        for k in (i, i + 1):
            loads[k].wait()
            if k + 3 < 8:
                loads[k + 3].start()
        part = slice(i * tile, (i + 2) * tile)
        logit_ref[part, :] = jnp.dot(held[part, :], normed[...], preferred_element_type=f32)


def head_forward(own, other, gain, head):
    vocab, width = head.shape
    return pl.pallas_call(
        head_kernel,
        in_specs=[VECTORS] * 3 + [FAR],
        out_specs=[VECTORS] * 4,
        out_shape=(
            jax.ShapeDtypeStruct((vocab, HALF), f32),
            jax.ShapeDtypeStruct((8, HALF), f32),
            jax.ShapeDtypeStruct((ROWS, width), bf16),
            jax.ShapeDtypeStruct((vocab, width), bf16),
        ),
        scratch_shapes=[
            pltpu.VMEM((HALF, width), f32),
            pltpu.VMEM((width, HALF), bf16),
            pltpu.SemaphoreType.DMA((8,)),
        ],
        compiler_params=pltpu.CompilerParams(vmem_limit_bytes=24 * MIB),
        cost_estimate=pl.CostEstimate(
            flops=4 * HALF * vocab * width, bytes_accessed=2 * vocab * width, transcendentals=0
        ),
        name="head_forward",
    )(own, other, gain, head)


def stat_kernel(
    length_ref, logit_ref, scale_ref, target_ref, mask_ref, slot_ref, *refs
):
    spares = refs[:4]
    chosen_ref, stat_ref, side_ref, pool, pool_sems = refs[4:]
    moves = [
        pltpu.make_async_copy(spares[-dx % 4].at[dy], pool.at[k], pool_sems.at[k])
        for k, (dx, dy) in enumerate(PLACES)
    ]
    for copy in moves:
        copy.start()
    for copy in moves:
        copy.wait()
    have = have_here(length_ref[0])
    row = lax.broadcasted_iota(jnp.int32, (HALF, 384), 0)
    pick = (row.astype(f32) == slot_ref[0:1, 0:384]).astype(bf16)
    spare = pool[:, 0:SPARE, :].reshape(384, pool.shape[2])
    moved = jnp.dot(pick, spare, preferred_element_type=f32)
    kept = lax.broadcasted_iota(jnp.int32, moved.shape, 0) < have
    chosen = jnp.transpose(jnp.where(kept, target_ref[...].astype(f32), moved))
    chosen_ref[...] = chosen
    column = lax.broadcasted_iota(jnp.int32, (1, 384), 1)
    mask_pool = seq_pool = jnp.zeros((1, 384), f32)
    counts = []
    for k, place in enumerate(PLACES):
        mine = (column >= SPARE * k) & (column < SPARE * (k + 1))
        facts = pool[k, SPARE : SPARE + 16, :].astype(f32)
        mask_pool = jnp.where(mine, facts[0:1, 0:384], mask_pool)
        seq_pool = jnp.where(mine, (group_at(*place) // 2).astype(f32), seq_pool)
        counts.append(facts[1:2, 0:HALF])
    none = jnp.zeros((6, 384), f32)
    traits = lax.dot_general(
        jnp.concatenate([mask_pool, seq_pool, none], axis=0).astype(bf16), pick, (((1,), (1,)), ((), ())), preferred_element_type=f32
    )
    lane = lax.broadcasted_iota(jnp.int32, (1, HALF), 1)
    masked = (mask_ref[...] == 1).astype(f32)
    valid = jnp.where(lane < have, masked, traits[0:1])
    valid = jnp.where(lane < ROWS, valid, 0.0)
    sequence = jnp.where(lane < have, lax.axis_index("x").astype(f32), traits[1:2])
    nothing = jnp.zeros((1, HALF), f32)
    side_ref[...] = jnp.concatenate(
        [scale_ref[0:1], valid, sequence, sum(counts), counts[0] + counts[1]] + [nothing] * 3, axis=0
    )

    top_t = jnp.max(chosen, axis=0, keepdims=True)
    pow_t = jnp.exp(chosen - top_t)
    sum_t = jnp.sum(pow_t, axis=0, keepdims=True)
    dot_t = jnp.sum(pow_t * chosen, axis=0, keepdims=True)
    logits = logit_ref[...]
    top_d = jnp.max(logits, axis=0, keepdims=True)
    pow_d = jnp.exp(logits - top_d)
    stat_ref[...] = jnp.concatenate(
        [
            top_t,
            sum_t,
            dot_t,
            jnp.sum(pow_t * logits, axis=0, keepdims=True),
            top_d,
            jnp.sum(pow_d, axis=0, keepdims=True),
            jnp.sum(pow_d * logits, axis=0, keepdims=True),
            nothing,
        ],
        axis=0,
    )


def row_stats(lengths, logits, scales, target, loss_mask, slots, spares):
    vocab = logits.shape[0]
    return pl.pallas_call(
        stat_kernel,
        in_specs=[SCALARS] + [VECTORS] * 5 + [FAR] * 4,
        out_specs=[VECTORS] * 3,
        out_shape=(
            jax.ShapeDtypeStruct((vocab, HALF), f32),
            jax.ShapeDtypeStruct((8, HALF), f32),
            jax.ShapeDtypeStruct((8, HALF), f32),
        ),
        scratch_shapes=[
            pltpu.VMEM((GROUPS, SPARE + 16, vocab), bf16),
            pltpu.SemaphoreType.DMA((GROUPS,)),
        ],
        compiler_params=pltpu.CompilerParams(vmem_limit_bytes=16 * MIB),
        name="row_stats",
    )(lengths, logits, scales, target, loss_mask, slots, *spares)


def back_kernel(
    every_ref, logit_ref, chosen_ref, side_ref, gain_ref, united_ref, head_ref,
    mine_ref, other_ref,
):
    width = gain_ref.shape[1]
    every = every_ref[...]
    max_t = jnp.max(every[:, 0:1], axis=0)
    scale_t = jnp.exp(every[:, 0:1] - max_t[None])
    sum_t = jnp.sum(every[:, 1:2] * scale_t, axis=0)
    mean_tt = jnp.sum(every[:, 2:3] * scale_t, axis=0) / sum_t
    mean_tl = jnp.sum(every[:, 3:4] * scale_t, axis=0) / sum_t
    max_d = jnp.max(every[:, 4:5], axis=0)
    scale_d = jnp.exp(every[:, 4:5] - max_d[None])
    sum_d = jnp.sum(every[:, 5:6] * scale_d, axis=0)
    mean_dl = jnp.sum(every[:, 6:7] * scale_d, axis=0) / sum_d
    log_t = max_t + jnp.log(sum_t)
    log_d = max_d + jnp.log(sum_d)
    row_scale, valid, sequence = side_ref[0:1], side_ref[1:2], side_ref[2:3]
    kl = (mean_tt - mean_tl - log_t + log_d) * valid
    row = lax.broadcasted_iota(jnp.int32, (8, HALF), 0)
    sums = jnp.sum(jnp.where(row.astype(f32) == sequence, kl, 0.0), axis=1, keepdims=True)
    sums = jnp.broadcast_to(sums, (8, HALF))
    high = sums.astype(bf16).astype(f32)
    middle = (sums - high).astype(bf16).astype(f32)
    column = lax.broadcasted_iota(jnp.int32, (8, HALF), 1)
    third = jnp.where(column < 96, sums - high - middle, 0.0)
    sums = jnp.where(column < 32, high, jnp.where(column < 64, middle, third))

    weight = valid * row_scale
    grad = weight * (jnp.exp(logit_ref[...] - log_d) - jnp.exp(chosen_ref[...] - log_t))
    grad = jnp.transpose(grad)[0:ROWS].astype(bf16)
    lane = lax.broadcasted_iota(jnp.int32, (1, HALF), 1)
    share = ROWS // 16
    index = lax.axis_index(("z", "yl", "c"))
    mine = (lane >= index * share) & (lane < (index + 1) * share)
    cubic = jnp.where(mine, weight * row_scale * (mean_dl - mean_tl) / width, 0.0)
    cubic = jnp.transpose(jnp.broadcast_to(cubic, (HALF, HALF)))[0:ROWS, 0:1]
    for g in range(GROUPS):
        part = slice(g * 1024, (g + 1) * 1024)
        block = jnp.dot(grad, head_ref[:, part], preferred_element_type=f32)
        block = block * gain_ref[:, part] - cubic * united_ref[:, part].astype(f32)
        split_by_core(
            block, lax.axis_index("c") == 0, mine_ref.at[g], other_ref.at[g], sums
        )


def head_backward(every, logits, chosen, side, gain, united, head):
    return pl.pallas_call(
        back_kernel,
        in_specs=[VECTORS] * 7,
        out_specs=[VECTORS] * 2,
        out_shape=(
            jax.ShapeDtypeStruct((GROUPS, 8, PIECE + 8, 128), bf16),
            jax.ShapeDtypeStruct((GROUPS, 8, PIECE + 8, 128), bf16),
        ),
        compiler_params=pltpu.CompilerParams(vmem_limit_bytes=24 * MIB),
        name="head_backward",
    )(every, logits, chosen, side, gain, united, head)


def assemble(grad_ref, wide, grads):
    for k, place in enumerate(PLACES):
        group = group_at(*place)
        for j in range(8):
            wide[k * PIECE : (k + 1) * PIECE, j * 128 : (j + 1) * 128] = grad_ref[
                j, group
            ].astype(f32)
    grads[...] = wide[...].astype(bf16)


def near_kernel(grad_ref, rows_ref, out_ref, wide, grads):
    assemble(grad_ref, wide, grads)
    for s in range(3):
        out_ref[s] = lax.dot_general(
            rows_ref[s], grads[...], (((0,), (0,)), ((), ())), preferred_element_type=f32
        )


def far_kernel(side_ref, grad_ref, rows_ref, near_ref, out_ref, wide, grads, done, sems):
    assemble(grad_ref, wide, grads)
    factor = (2 * HALF) / jnp.maximum(side_ref[3:4, 0:1], 1.0)
    copies = []
    for s in range(3):
        for i in range(2):
            part = slice(i * 256, (i + 1) * 256)
            done[s, part, :] = factor * (
                near_ref[s, part, :]
                + lax.dot_general(
                    rows_ref[s, :, part],
                    grads[...],
                    (((0,), (0,)), ((), ())),
                    preferred_element_type=f32,
                )
            )
            copies.append(
                pltpu.make_async_copy(
                    done.at[s, pl.ds(i * 256, 256)],
                    out_ref.at[s, pl.ds(i * 256, 256)],
                    sems.at[2 * s + i],
                )
            )
            copies[-1].start()
    for copy in copies:
        copy.wait()


def near_gradient(own, rows):
    total = GROUPS * PIECE
    return pl.pallas_call(
        near_kernel,
        in_specs=[VECTORS] * 2,
        out_specs=VECTORS,
        out_shape=jax.ShapeDtypeStruct((3, 512, 1024), f32),
        scratch_shapes=[pltpu.VMEM((total, 1024), f32), pltpu.VMEM((total, 1024), bf16)],
        compiler_params=pltpu.CompilerParams(vmem_limit_bytes=16 * MIB),
        cost_estimate=pl.CostEstimate(
            flops=6 * total * 512 * 1024, bytes_accessed=6 * MIB, transcendentals=0
        ),
        name="near_gradient",
    )(own, rows)


def weight_gradient(side, other, rows, near):
    total = GROUPS * PIECE
    return pl.pallas_call(
        far_kernel,
        in_specs=[VECTORS] * 4,
        out_specs=FAR,
        out_shape=jax.ShapeDtypeStruct((3, 512, 1024), f32),
        scratch_shapes=[
            pltpu.VMEM((total, 1024), f32),
            pltpu.VMEM((total, 1024), bf16),
            pltpu.VMEM((3, 512, 1024), f32),
            pltpu.SemaphoreType.DMA((6,)),
        ],
        compiler_params=pltpu.CompilerParams(vmem_limit_bytes=24 * MIB),
        name="weight_gradient",
    )(side, other, rows, near)


def sum_kernel(piece_ref, out_ref, extra_ref):
    extra = jnp.zeros((8, 128), f32)
    for g in range(GROUPS):
        total = jnp.zeros((PIECE, 128), f32)
        for j in range(8):
            total = total + piece_ref[g * 8 + j, 0:PIECE, :].astype(f32)
        for k in range(8):
            out_ref[k, g] = total.astype(bf16)
        if piece_ref.shape[1] > PIECE:
            extra = extra + piece_ref[g * 8].astype(f32)[PIECE : PIECE + 8]
    extra_ref[...] = extra


def gather_sum(mine, other):
    pair = (mine.astype(f32) + swap(other, "c", 1, 2).astype(f32)).astype(bf16)
    received = lax.all_to_all(pair.reshape((64,) + pair.shape[2:]), CHIPS, 0, 0, tiled=True)
    copies, extra = pl.pallas_call(
        sum_kernel,
        in_specs=[VECTORS],
        out_specs=[VECTORS] * 2,
        out_shape=(
            jax.ShapeDtypeStruct((8, GROUPS, PIECE, 128), bf16),
            jax.ShapeDtypeStruct((8, 128), f32),
        ),
        compiler_params=pltpu.CompilerParams(vmem_limit_bytes=8 * MIB),
        name="sum_pieces",
    )(received)
    return copies, extra


def route(value, dx, dy):
    pairs = [(p * 2 + q, (p + dx) % 4 * 2 + (q ^ dy)) for p in range(4) for q in range(2)]
    return lax.ppermute(value, GROUP, pairs)


def local(captured, target_logits, unite_weight, norm_gain, head_weight, lengths, loss_mask):
    width = norm_gain.shape[0]
    own = captured.reshape(3, HALF, 512)
    target = target_logits.reshape(HALF, -1)
    far = route(own, 2, 0)
    over = route(own, 0, 1)
    right = route(own, 3, 0)
    left = route(own, 1, 0)
    far, near_target, later = lax.optimization_barrier((far, target, lengths))
    over_far = route(far, 0, 1)
    over_right = route(over, 3, 0)
    over_left = route(over, 1, 0)
    spare = spare_facts(lengths, loss_mask, near_target)
    pair = jnp.stack([spare, route(spare, 0, 1)])
    left, right, weight = lax.optimization_barrier((left, right, unite_weight))
    weight, near = stage(weight, own)
    wide_length = jnp.broadcast_to(later.astype(f32), (8, HALF))
    all_lengths = [wide_length, route(wide_length, 1, 0), route(wide_length, 3, 0)]
    over_far, pair = lax.optimization_barrier((over_far, pair))
    blocks = [near, over, left, right, far, over_left, over_right, over_far]
    near_rows, far_rows, mine, other, slots = unite(blocks, all_lengths, weight)

    copies, _ = gather_sum(mine, other)
    copies, pair = lax.optimization_barrier((copies, pair))
    spares = [pair] + [route(pair, dx, 0) for dx in range(1, 4)]
    own_united = lax.all_to_all(copies, RING, 0, 0, tiled=True)
    own_united, spares[1], spares[3] = lax.optimization_barrier(
        (own_united, spares[1], spares[3])
    )
    other_united = swap(own_united, "c", 1, 2)
    gain = norm_gain.reshape(1, width)
    logits, scales, united, held = head_forward(own_united, other_united, gain, head_weight)
    chosen, stats, side = row_stats(
        lengths, logits, scales, target, loss_mask, slots, spares
    )
    every = spread(stats, ("z", "yl", "c"), 16)
    mine, other = head_backward(every, logits, chosen, side, gain, united, held)
    copies, sums = gather_sum(mine, other)
    own_grad = lax.all_to_all(copies, RING, 0, 0, tiled=True)
    seq_sum = jnp.sum(
        jnp.where(lax.iota(jnp.int32, GROUPS)[:, None] == lax.axis_index("x"), sums, 0.0)
    )
    seq_kl = (seq_sum / 32.0 / jnp.maximum(side[4, 0], 1.0)).reshape(1)
    own_grad, seq_kl = lax.optimization_barrier((own_grad, seq_kl))
    other_grad = swap(own_grad, "c", 1, 2)
    near_part = near_gradient(own_grad, near_rows)
    unite_grad = weight_gradient(side, other_grad, far_rows, near_part)
    return (seq_kl, unite_grad)


def solution(mesh):
    fine = Mesh(mesh.devices.reshape(4, 2, 4, 2, 2), ALL)
    tensor = ("z", "yl", "c")
    placed = (
        P(None, "x", "yh", tensor),
        P("x", "yh", tensor),
        P(None, tensor, GROUP),
        P(),
        P(tensor, None),
        P("x"),
        P("x", "yh"),
    )
    return jax.shard_map(
        local,
        mesh=fine,
        in_specs=placed,
        out_specs=(P("x"), P(None, tensor, GROUP)),
        check_vma=False,
    )
```

```python
import functools

import jax
import jax.numpy as jnp
from jax import lax
from jax.experimental import pallas as pl
from jax.experimental.pallas import tpu as pltpu
from jax.sharding import Mesh, PartitionSpec as P

NORM_EPS = 1e-05
GROUP = ("x", "yh")
RING = ("z", "yl")
CHIPS = ("x", "yh", "z", "yl")
ALL = CHIPS + ("c",)
PLACES = [(0, 0), (0, 1), (3, 0), (1, 0), (2, 0), (3, 1), (1, 1), (2, 1)]
GROUPS = 8
HALF = 128
ROWS = 80
SPARE = HALF - ROWS
PIECE = ROWS // 2
MIB = 1 << 20
f32, bf16 = jnp.float32, jnp.bfloat16
SCALARS = pl.BlockSpec(memory_space=pltpu.SMEM)
VECTORS = pl.BlockSpec(memory_space=pltpu.VMEM)
FAR = pl.BlockSpec(memory_space=pltpu.HBM)


def group_at(dx, dy):
    return lax.rem(lax.axis_index("x") + dx, 4) * 2 + lax.rem(lax.axis_index("yh") + dy, 2)


def have_here(length):
    return jnp.clip(length - lax.axis_index("yh") * HALF, 0, HALF)


def spread(value, axes, count):
    return lax.all_to_all(
        jnp.broadcast_to(value[None], (count,) + value.shape), axes, 0, 0, tiled=True
    )


def swap(value, axis, bit, count):
    return lax.ppermute(value, axis, [(i, i ^ bit) for i in range(count)])


def spare_kernel(length_ref, mask_ref, target_ref, spare_ref):
    vocab = target_ref.shape[1]
    masked = (mask_ref[...] == 1).astype(f32)
    near = lax.broadcasted_iota(jnp.int32, (1, HALF), 1) < have_here(length_ref[0])
    count = jnp.sum(jnp.where(near, masked, 0.0), axis=1, keepdims=True)
    place = lax.broadcasted_iota(jnp.int32, (HALF, vocab), 0) - ROWS
    column = lax.broadcasted_iota(jnp.int32, (HALF, vocab), 1)
    tiled = jnp.zeros((HALF, vocab), f32)
    for k in range(GROUPS):
        tiled = jnp.where((column - SPARE * k == place) & (place >= 0), 1.0, tiled)
    repeated = jnp.dot(
        jnp.broadcast_to(masked, (8, HALF)).astype(bf16),
        tiled.astype(bf16),
        preferred_element_type=f32,
    )[0:1]
    row = lax.broadcasted_iota(jnp.int32, (16, vocab), 0)
    facts = jnp.where(row == 0, repeated, jnp.where(row == 1, count, 0.0))
    spare_ref[0:SPARE, :] = target_ref[ROWS:HALF, :]
    spare_ref[SPARE : SPARE + 16, :] = facts.astype(bf16)


def spare_facts(lengths, loss_mask, target):
    return pl.pallas_call(
        spare_kernel,
        in_specs=[SCALARS, VECTORS, VECTORS],
        out_specs=VECTORS,
        out_shape=jax.ShapeDtypeStruct((SPARE + 16, target.shape[1]), bf16),
        compiler_params=pltpu.CompilerParams(vmem_limit_bytes=8 * MIB),
        name="spare_facts",
    )(lengths, loss_mask, target)


def stage_kernel(hbm_weight, hbm_cap, weight_ref, cap_ref, sems):
    copies = [
        pltpu.make_async_copy(hbm_weight, weight_ref, sems.at[0]),
        pltpu.make_async_copy(hbm_cap, cap_ref, sems.at[1]),
    ]
    for copy in copies:
        copy.start()
    for copy in copies:
        copy.wait()


def stage(weight, captured):
    return pl.pallas_call(
        stage_kernel,
        in_specs=[FAR, FAR],
        out_specs=[VECTORS] * 2,
        out_shape=(
            jax.ShapeDtypeStruct(weight.shape, bf16),
            jax.ShapeDtypeStruct(captured.shape, bf16),
        ),
        scratch_shapes=[pltpu.SemaphoreType.DMA((2,))],
        compiler_params=pltpu.CompilerParams(vmem_limit_bytes=8 * MIB),
        name="stage",
    )(weight, captured)


def split_by_core(block, first, mine_ref, other_ref, extra=None):
    for j in range(8):
        upper = block[0:PIECE, j * 128 : (j + 1) * 128]
        lower = block[PIECE:ROWS, j * 128 : (j + 1) * 128]
        mine = jnp.where(first, upper, lower)
        other = jnp.where(first, lower, upper)
        if extra is not None:
            mine = jnp.concatenate([mine, extra], axis=0)
            other = jnp.concatenate([other, jnp.zeros_like(extra)], axis=0)
        mine_ref[j] = mine.astype(bf16)
        other_ref[j] = other.astype(bf16)


def unite_kernel(*refs):
    blocks, length_refs = refs[:GROUPS], refs[GROUPS : GROUPS + 3]
    weight_ref, near_rows_ref, far_rows_ref, mine_ref, other_ref, slot_ref = refs[GROUPS + 3 :]
    lengths = [jnp.broadcast_to(ref[0:1, 0:1], (1, 512)) for ref in length_refs]
    lengths = {0: lengths[0], 3: lengths[1], 1: lengths[2], 2: GROUPS * ROWS - sum(lengths)}
    first = lax.axis_index("c") == 0
    groups = [group_at(*place) for place in PLACES]
    lane = lax.broadcasted_iota(jnp.int32, (1, 512), 1).astype(f32)
    have = [
        jnp.clip(
            lengths[dx]
            - lax.rem(lax.axis_index("yh") + dy, 2).astype(f32) * HALF,
            0.0,
            float(HALF),
        )
        for dx, dy in PLACES
    ]
    more = [jnp.maximum(h - ROWS, 0.0) for h in have]
    less = [jnp.maximum(ROWS - h, 0.0) for h in have]

    def before(amounts, k):
        total = jnp.zeros((1, 512), f32)
        for m in range(GROUPS):
            if m != k:
                total = total + amounts[m] * (groups[m] < groups[k]).astype(f32)
        return total

    order = jnp.full((1, 512), -1.0, f32)
    for k in range(GROUPS):
        place = lane - SPARE * k
        mine = (place >= 0) & (place < SPARE)
        order = jnp.where(mine & (place < have[k] - ROWS), before(more, k) + place, order)
    slot = jnp.full((1, 512), -1.0, f32)
    for k in range(GROUPS):
        offset = order - before(less, k)
        mine = (order >= 0) & (offset >= 0) & (offset < ROWS - have[k])
        slot = jnp.where(mine, ROWS * k + have[k] + offset, slot)
    slot_ref[...] = jnp.broadcast_to(slot, (8, 512))
    for half in range(2):
        row = lax.broadcasted_iota(jnp.int32, (4 * ROWS, 384), 0) + half * 4 * ROWS
        pick = (row.astype(f32) == slot[:, :384]).astype(bf16)
        total = None
        for s in range(3):
            pool = jnp.concatenate([block[s, ROWS:HALF, :] for block in blocks], axis=0)
            moved = jnp.dot(pick, pool, preferred_element_type=f32)
            kept = []
            for k in range(4 * half, 4 * half + 4):
                own = blocks[k][s, 0:ROWS, :].astype(f32)
                within = lax.broadcasted_iota(jnp.int32, (ROWS, 512), 0).astype(f32) < have[k]
                base = (k - 4 * half) * ROWS
                kept.append(jnp.where(within, own, moved[base : base + ROWS]))
            upper = jnp.concatenate([rows[0:PIECE] for rows in kept], axis=0)
            lower = jnp.concatenate([rows[PIECE:ROWS] for rows in kept], axis=0)
            part = pl.ds(half * 4 * PIECE, 4 * PIECE)
            near_rows_ref[s, part, :] = jnp.where(first, upper, lower).astype(bf16)
            far_rows_ref[s, part, :] = jnp.where(first, lower, upper).astype(bf16)
            rows = jnp.concatenate(kept, axis=0).astype(bf16)
            term = jnp.dot(rows, weight_ref[s], preferred_element_type=f32)
            total = term if total is None else total + term
        for k in range(4):
            group = groups[4 * half + k]
            split_by_core(
                total[k * ROWS : (k + 1) * ROWS], first, mine_ref.at[group], other_ref.at[group]
            )


def unite(blocks, lengths, weight):
    return pl.pallas_call(
        unite_kernel,
        in_specs=[VECTORS] * (GROUPS + 4),
        out_specs=[VECTORS] * 5,
        out_shape=(
            jax.ShapeDtypeStruct((3, GROUPS * PIECE, 512), bf16),
            jax.ShapeDtypeStruct((3, GROUPS * PIECE, 512), bf16),
            jax.ShapeDtypeStruct((GROUPS, 8, PIECE, 128), bf16),
            jax.ShapeDtypeStruct((GROUPS, 8, PIECE, 128), bf16),
            jax.ShapeDtypeStruct((8, 512), f32),
        ),
        compiler_params=pltpu.CompilerParams(vmem_limit_bytes=24 * MIB),
        name="unite",
    )(*blocks, *lengths, weight)


def head_kernel(
    own_ref, other_ref, gain_ref, head_ref,
    logit_ref, scale_ref, united_ref, held, wide, normed, sems,
):
    width = wide.shape[1]
    tile = head_ref.shape[0] // 8
    loads = [
        pltpu.make_async_copy(
            head_ref.at[pl.ds(i * tile, tile)], held.at[pl.ds(i * tile, tile)], sems.at[i]
        )
        for i in range(8)
    ]
    for copy in loads[:3]:
        copy.start()

    first = lax.axis_index("c") == 0
    wide[ROWS:HALF, :] = jnp.zeros((HALF - ROWS, width), f32)
    for g in range(GROUPS):
        for j in range(8):
            column = (g * 8 + j) * 128
            a = own_ref[j, g].astype(f32)
            b = other_ref[j, g].astype(f32)
            wide[0:PIECE, column : column + 128] = jnp.where(first, a, b)
            wide[PIECE:ROWS, column : column + 128] = jnp.where(first, b, a)
    square = jnp.zeros((HALF, 1), f32)
    for g in range(GROUPS):
        values = wide[:, g * 1024 : (g + 1) * 1024]
        square = square + jnp.sum(values * values, axis=1, keepdims=True)
    scale = lax.rsqrt(square / width + NORM_EPS)
    for g in range(GROUPS):
        part = slice(g * 1024, (g + 1) * 1024)
        values = wide[:, part]
        united_ref[:, part] = values[0:ROWS].astype(bf16)
        normed[part, :] = jnp.transpose(values * scale * gain_ref[:, part]).astype(bf16)

    scale_ref[...] = jnp.transpose(jnp.broadcast_to(scale, (HALF, HALF)))[0:8]
    for i in range(8):
        loads[i].wait()
        if i + 3 < 8:
            loads[i + 3].start()
        part = slice(i * tile, (i + 1) * tile)
        logit_ref[part, :] = jnp.dot(held[part, :], normed[...], preferred_element_type=f32)


def head_forward(own, other, gain, head):
    vocab, width = head.shape
    return pl.pallas_call(
        head_kernel,
        in_specs=[VECTORS] * 3 + [FAR],
        out_specs=[VECTORS] * 4,
        out_shape=(
            jax.ShapeDtypeStruct((vocab, HALF), f32),
            jax.ShapeDtypeStruct((8, HALF), f32),
            jax.ShapeDtypeStruct((ROWS, width), bf16),
            jax.ShapeDtypeStruct((vocab, width), bf16),
        ),
        scratch_shapes=[
            pltpu.VMEM((HALF, width), f32),
            pltpu.VMEM((width, HALF), bf16),
            pltpu.SemaphoreType.DMA((8,)),
        ],
        compiler_params=pltpu.CompilerParams(vmem_limit_bytes=24 * MIB),
        cost_estimate=pl.CostEstimate(
            flops=4 * HALF * vocab * width, bytes_accessed=2 * vocab * width, transcendentals=0
        ),
        name="head_forward",
    )(own, other, gain, head)


def stat_kernel(
    length_ref, logit_ref, scale_ref, target_ref, mask_ref, slot_ref, *refs
):
    spares = refs[:4]
    chosen_ref, stat_ref, side_ref, pool, pool_sems = refs[4:]
    moves = [
        pltpu.make_async_copy(spares[-dx % 4].at[dy], pool.at[k], pool_sems.at[k])
        for k, (dx, dy) in enumerate(PLACES)
    ]
    for copy in moves:
        copy.start()
    for copy in moves:
        copy.wait()
    have = have_here(length_ref[0])
    row = lax.broadcasted_iota(jnp.int32, (HALF, 384), 0)
    pick = (row.astype(f32) == slot_ref[0:1, 0:384]).astype(bf16)
    spare = pool[:, 0:SPARE, :].reshape(384, pool.shape[2])
    moved = jnp.dot(pick, spare, preferred_element_type=f32)
    kept = lax.broadcasted_iota(jnp.int32, moved.shape, 0) < have
    chosen = jnp.transpose(jnp.where(kept, target_ref[...].astype(f32), moved))
    chosen_ref[...] = chosen
    column = lax.broadcasted_iota(jnp.int32, (1, 384), 1)
    mask_pool = seq_pool = jnp.zeros((1, 384), f32)
    counts = []
    for k, place in enumerate(PLACES):
        mine = (column >= SPARE * k) & (column < SPARE * (k + 1))
        facts = pool[k, SPARE : SPARE + 16, :].astype(f32)
        mask_pool = jnp.where(mine, facts[0:1, 0:384], mask_pool)
        seq_pool = jnp.where(mine, (group_at(*place) // 2).astype(f32), seq_pool)
        counts.append(facts[1:2, 0:HALF])
    none = jnp.zeros((6, 384), f32)
    traits = lax.dot_general(
        jnp.concatenate([mask_pool, seq_pool, none], axis=0).astype(bf16), pick, (((1,), (1,)), ((), ())), preferred_element_type=f32
    )
    lane = lax.broadcasted_iota(jnp.int32, (1, HALF), 1)
    masked = (mask_ref[...] == 1).astype(f32)
    valid = jnp.where(lane < have, masked, traits[0:1])
    valid = jnp.where(lane < ROWS, valid, 0.0)
    sequence = jnp.where(lane < have, lax.axis_index("x").astype(f32), traits[1:2])
    nothing = jnp.zeros((1, HALF), f32)
    side_ref[...] = jnp.concatenate(
        [scale_ref[0:1], valid, sequence, sum(counts), counts[0] + counts[1]] + [nothing] * 3, axis=0
    )

    top_t = jnp.max(chosen, axis=0, keepdims=True)
    pow_t = jnp.exp(chosen - top_t)
    sum_t = jnp.sum(pow_t, axis=0, keepdims=True)
    dot_t = jnp.sum(pow_t * chosen, axis=0, keepdims=True)
    logits = logit_ref[...]
    top_d = jnp.max(logits, axis=0, keepdims=True)
    pow_d = jnp.exp(logits - top_d)
    stat_ref[...] = jnp.concatenate(
        [
            top_t,
            sum_t,
            dot_t,
            jnp.sum(pow_t * logits, axis=0, keepdims=True),
            top_d,
            jnp.sum(pow_d, axis=0, keepdims=True),
            jnp.sum(pow_d * logits, axis=0, keepdims=True),
            nothing,
        ],
        axis=0,
    )


def row_stats(lengths, logits, scales, target, loss_mask, slots, spares):
    vocab = logits.shape[0]
    return pl.pallas_call(
        stat_kernel,
        in_specs=[SCALARS] + [VECTORS] * 5 + [FAR] * 4,
        out_specs=[VECTORS] * 3,
        out_shape=(
            jax.ShapeDtypeStruct((vocab, HALF), f32),
            jax.ShapeDtypeStruct((8, HALF), f32),
            jax.ShapeDtypeStruct((8, HALF), f32),
        ),
        scratch_shapes=[
            pltpu.VMEM((GROUPS, SPARE + 16, vocab), bf16),
            pltpu.SemaphoreType.DMA((GROUPS,)),
        ],
        compiler_params=pltpu.CompilerParams(vmem_limit_bytes=16 * MIB),
        name="row_stats",
    )(lengths, logits, scales, target, loss_mask, slots, *spares)


def back_kernel(
    every_ref, logit_ref, chosen_ref, side_ref, gain_ref, united_ref, head_ref,
    mine_ref, other_ref,
):
    width = gain_ref.shape[1]
    every = every_ref[...]
    max_t = jnp.max(every[:, 0:1], axis=0)
    scale_t = jnp.exp(every[:, 0:1] - max_t[None])
    sum_t = jnp.sum(every[:, 1:2] * scale_t, axis=0)
    mean_tt = jnp.sum(every[:, 2:3] * scale_t, axis=0) / sum_t
    mean_tl = jnp.sum(every[:, 3:4] * scale_t, axis=0) / sum_t
    max_d = jnp.max(every[:, 4:5], axis=0)
    scale_d = jnp.exp(every[:, 4:5] - max_d[None])
    sum_d = jnp.sum(every[:, 5:6] * scale_d, axis=0)
    mean_dl = jnp.sum(every[:, 6:7] * scale_d, axis=0) / sum_d
    log_t = max_t + jnp.log(sum_t)
    log_d = max_d + jnp.log(sum_d)
    row_scale, valid, sequence = side_ref[0:1], side_ref[1:2], side_ref[2:3]
    kl = (mean_tt - mean_tl - log_t + log_d) * valid
    row = lax.broadcasted_iota(jnp.int32, (8, HALF), 0)
    sums = jnp.sum(jnp.where(row.astype(f32) == sequence, kl, 0.0), axis=1, keepdims=True)
    sums = jnp.broadcast_to(sums, (8, HALF))
    high = sums.astype(bf16).astype(f32)
    middle = (sums - high).astype(bf16).astype(f32)
    column = lax.broadcasted_iota(jnp.int32, (8, HALF), 1)
    third = jnp.where(column < 96, sums - high - middle, 0.0)
    sums = jnp.where(column < 32, high, jnp.where(column < 64, middle, third))

    weight = valid * row_scale
    grad = weight * (jnp.exp(logit_ref[...] - log_d) - jnp.exp(chosen_ref[...] - log_t))
    grad = jnp.transpose(grad)[0:ROWS].astype(bf16)
    lane = lax.broadcasted_iota(jnp.int32, (1, HALF), 1)
    share = ROWS // 16
    index = lax.axis_index(("z", "yl", "c"))
    mine = (lane >= index * share) & (lane < (index + 1) * share)
    cubic = jnp.where(mine, weight * row_scale * (mean_dl - mean_tl) / width, 0.0)
    cubic = jnp.transpose(jnp.broadcast_to(cubic, (HALF, HALF)))[0:ROWS, 0:1]
    for g in range(GROUPS):
        part = slice(g * 1024, (g + 1) * 1024)
        block = jnp.dot(grad, head_ref[:, part], preferred_element_type=f32)
        block = block * gain_ref[:, part] - cubic * united_ref[:, part].astype(f32)
        split_by_core(
            block, lax.axis_index("c") == 0, mine_ref.at[g], other_ref.at[g], sums
        )


def head_backward(every, logits, chosen, side, gain, united, head):
    return pl.pallas_call(
        back_kernel,
        in_specs=[VECTORS] * 7,
        out_specs=[VECTORS] * 2,
        out_shape=(
            jax.ShapeDtypeStruct((GROUPS, 8, PIECE + 8, 128), bf16),
            jax.ShapeDtypeStruct((GROUPS, 8, PIECE + 8, 128), bf16),
        ),
        compiler_params=pltpu.CompilerParams(vmem_limit_bytes=24 * MIB),
        name="head_backward",
    )(every, logits, chosen, side, gain, united, head)


def assemble(grad_ref, wide, grads):
    for k, place in enumerate(PLACES):
        group = group_at(*place)
        for j in range(8):
            wide[k * PIECE : (k + 1) * PIECE, j * 128 : (j + 1) * 128] = grad_ref[
                j, group
            ].astype(f32)
    grads[...] = wide[...].astype(bf16)


def near_kernel(grad_ref, rows_ref, out_ref, wide, grads):
    assemble(grad_ref, wide, grads)
    for s in range(3):
        out_ref[s] = lax.dot_general(
            rows_ref[s], grads[...], (((0,), (0,)), ((), ())), preferred_element_type=f32
        )


def far_kernel(side_ref, grad_ref, rows_ref, near_ref, out_ref, wide, grads, done, sems):
    assemble(grad_ref, wide, grads)
    factor = (2 * HALF) / jnp.maximum(side_ref[3:4, 0:1], 1.0)
    copies = []
    for s in range(3):
        for i in range(2):
            part = slice(i * 256, (i + 1) * 256)
            done[s, part, :] = factor * (
                near_ref[s, part, :]
                + lax.dot_general(
                    rows_ref[s, :, part],
                    grads[...],
                    (((0,), (0,)), ((), ())),
                    preferred_element_type=f32,
                )
            )
            copies.append(
                pltpu.make_async_copy(
                    done.at[s, pl.ds(i * 256, 256)],
                    out_ref.at[s, pl.ds(i * 256, 256)],
                    sems.at[2 * s + i],
                )
            )
            copies[-1].start()
    for copy in copies:
        copy.wait()


def near_gradient(own, rows):
    total = GROUPS * PIECE
    return pl.pallas_call(
        near_kernel,
        in_specs=[VECTORS] * 2,
        out_specs=VECTORS,
        out_shape=jax.ShapeDtypeStruct((3, 512, 1024), f32),
        scratch_shapes=[pltpu.VMEM((total, 1024), f32), pltpu.VMEM((total, 1024), bf16)],
        compiler_params=pltpu.CompilerParams(vmem_limit_bytes=16 * MIB),
        cost_estimate=pl.CostEstimate(
            flops=6 * total * 512 * 1024, bytes_accessed=6 * MIB, transcendentals=0
        ),
        name="near_gradient",
    )(own, rows)


def weight_gradient(side, other, rows, near):
    total = GROUPS * PIECE
    return pl.pallas_call(
        far_kernel,
        in_specs=[VECTORS] * 4,
        out_specs=FAR,
        out_shape=jax.ShapeDtypeStruct((3, 512, 1024), f32),
        scratch_shapes=[
            pltpu.VMEM((total, 1024), f32),
            pltpu.VMEM((total, 1024), bf16),
            pltpu.VMEM((3, 512, 1024), f32),
            pltpu.SemaphoreType.DMA((6,)),
        ],
        compiler_params=pltpu.CompilerParams(vmem_limit_bytes=24 * MIB),
        name="weight_gradient",
    )(side, other, rows, near)


def sum_kernel(piece_ref, out_ref, extra_ref):
    extra = jnp.zeros((8, 128), f32)
    for g in range(GROUPS):
        total = jnp.zeros((PIECE, 128), f32)
        for j in range(8):
            total = total + piece_ref[g * 8 + j, 0:PIECE, :].astype(f32)
        for k in range(8):
            out_ref[k, g] = total.astype(bf16)
        if piece_ref.shape[1] > PIECE:
            extra = extra + piece_ref[g * 8].astype(f32)[PIECE : PIECE + 8]
    extra_ref[...] = extra


def gather_sum(mine, other):
    pair = (mine.astype(f32) + swap(other, "c", 1, 2).astype(f32)).astype(bf16)
    received = lax.all_to_all(pair.reshape((64,) + pair.shape[2:]), CHIPS, 0, 0, tiled=True)
    copies, extra = pl.pallas_call(
        sum_kernel,
        in_specs=[VECTORS],
        out_specs=[VECTORS] * 2,
        out_shape=(
            jax.ShapeDtypeStruct((8, GROUPS, PIECE, 128), bf16),
            jax.ShapeDtypeStruct((8, 128), f32),
        ),
        compiler_params=pltpu.CompilerParams(vmem_limit_bytes=8 * MIB),
        name="sum_pieces",
    )(received)
    return copies, extra


def route(value, dx, dy):
    pairs = [(p * 2 + q, (p + dx) % 4 * 2 + (q ^ dy)) for p in range(4) for q in range(2)]
    return lax.ppermute(value, GROUP, pairs)


def local(captured, target_logits, unite_weight, norm_gain, head_weight, lengths, loss_mask):
    width = norm_gain.shape[0]
    own = captured.reshape(3, HALF, 512)
    target = target_logits.reshape(HALF, -1)
    far = route(own, 2, 0)
    over = route(own, 0, 1)
    right = route(own, 3, 0)
    left = route(own, 1, 0)
    far, near_target, later = lax.optimization_barrier((far, target, lengths))
    over_far = route(far, 0, 1)
    over_right = route(over, 3, 0)
    over_left = route(over, 1, 0)
    spare = spare_facts(lengths, loss_mask, near_target)
    pair = jnp.stack([spare, route(spare, 0, 1)])
    left, right, weight = lax.optimization_barrier((left, right, unite_weight))
    weight, near = stage(weight, own)
    wide_length = jnp.broadcast_to(later.astype(f32), (8, HALF))
    all_lengths = [wide_length, route(wide_length, 1, 0), route(wide_length, 3, 0)]
    over_far, pair = lax.optimization_barrier((over_far, pair))
    blocks = [near, over, left, right, far, over_left, over_right, over_far]
    near_rows, far_rows, mine, other, slots = unite(blocks, all_lengths, weight)

    copies, _ = gather_sum(mine, other)
    copies, pair = lax.optimization_barrier((copies, pair))
    spares = [pair] + [route(pair, dx, 0) for dx in range(1, 4)]
    own_united = lax.all_to_all(copies, RING, 0, 0, tiled=True)
    own_united, spares[1], spares[3] = lax.optimization_barrier(
        (own_united, spares[1], spares[3])
    )
    other_united = swap(own_united, "c", 1, 2)
    gain = norm_gain.reshape(1, width)
    logits, scales, united, held = head_forward(own_united, other_united, gain, head_weight)
    chosen, stats, side = row_stats(
        lengths, logits, scales, target, loss_mask, slots, spares
    )
    every = spread(stats, ("z", "yl", "c"), 16)
    mine, other = head_backward(every, logits, chosen, side, gain, united, held)
    copies, sums = gather_sum(mine, other)
    own_grad = lax.all_to_all(copies, RING, 0, 0, tiled=True)
    seq_sum = jnp.sum(
        jnp.where(lax.iota(jnp.int32, GROUPS)[:, None] == lax.axis_index("x"), sums, 0.0)
    )
    seq_kl = (seq_sum / 32.0 / jnp.maximum(side[4, 0], 1.0)).reshape(1)
    own_grad, seq_kl = lax.optimization_barrier((own_grad, seq_kl))
    other_grad = swap(own_grad, "c", 1, 2)
    near_part = near_gradient(own_grad, near_rows)
    unite_grad = weight_gradient(side, other_grad, far_rows, near_part)
    return (seq_kl, unite_grad)


def solution(mesh):
    fine = Mesh(mesh.devices.reshape(4, 2, 4, 2, 2), ALL)
    tensor = ("z", "yl", "c")
    placed = (
        P(None, "x", "yh", tensor),
        P("x", "yh", tensor),
        P(None, tensor, GROUP),
        P(),
        P(tensor, None),
        P("x"),
        P("x", "yh"),
    )
    return jax.shard_map(
        local,
        mesh=fine,
        in_specs=placed,
        out_specs=(P("x"), P(None, tensor, GROUP)),
        check_vma=False,
    )
```

```python
import functools

import jax
import jax.numpy as jnp
from jax import lax
from jax.experimental import pallas as pl
from jax.experimental.pallas import tpu as pltpu
from jax.sharding import Mesh, PartitionSpec as P

NORM_EPS = 1e-05
GROUP = ("x", "yh")
RING = ("z", "yl")
CHIPS = ("x", "yh", "z", "yl")
ALL = CHIPS + ("c",)
PLACES = [(0, 0), (0, 1), (3, 0), (1, 0), (2, 0), (3, 1), (1, 1), (2, 1)]
GROUPS = 8
HALF = 128
ROWS = 80
SPARE = HALF - ROWS
PIECE = ROWS // 2
MIB = 1 << 20
f32, bf16 = jnp.float32, jnp.bfloat16
SCALARS = pl.BlockSpec(memory_space=pltpu.SMEM)
VECTORS = pl.BlockSpec(memory_space=pltpu.VMEM)
FAR = pl.BlockSpec(memory_space=pltpu.HBM)


def group_at(dx, dy):
    return lax.rem(lax.axis_index("x") + dx, 4) * 2 + lax.rem(lax.axis_index("yh") + dy, 2)


def have_here(length):
    return jnp.clip(length - lax.axis_index("yh") * HALF, 0, HALF)


def spread(value, axes, count):
    return lax.all_to_all(
        jnp.broadcast_to(value[None], (count,) + value.shape), axes, 0, 0, tiled=True
    )


def swap(value, axis, bit, count):
    return lax.ppermute(value, axis, [(i, i ^ bit) for i in range(count)])


def spare_kernel(length_ref, mask_ref, target_ref, spare_ref):
    vocab = target_ref.shape[1]
    masked = (mask_ref[...] == 1).astype(f32)
    near = lax.broadcasted_iota(jnp.int32, (1, HALF), 1) < have_here(length_ref[0])
    count = jnp.sum(jnp.where(near, masked, 0.0), axis=1, keepdims=True)
    place = lax.broadcasted_iota(jnp.int32, (HALF, vocab), 0) - ROWS
    column = lax.broadcasted_iota(jnp.int32, (HALF, vocab), 1)
    tiled = jnp.zeros((HALF, vocab), f32)
    for k in range(GROUPS):
        tiled = jnp.where((column - SPARE * k == place) & (place >= 0), 1.0, tiled)
    repeated = jnp.dot(
        jnp.broadcast_to(masked, (8, HALF)).astype(bf16),
        tiled.astype(bf16),
        preferred_element_type=f32,
    )[0:1]
    row = lax.broadcasted_iota(jnp.int32, (16, vocab), 0)
    facts = jnp.where(row == 0, repeated, jnp.where(row == 1, count, 0.0))
    spare_ref[0:SPARE, :] = target_ref[ROWS:HALF, :]
    spare_ref[SPARE : SPARE + 16, :] = facts.astype(bf16)


def spare_facts(lengths, loss_mask, target):
    return pl.pallas_call(
        spare_kernel,
        in_specs=[SCALARS, VECTORS, VECTORS],
        out_specs=VECTORS,
        out_shape=jax.ShapeDtypeStruct((SPARE + 16, target.shape[1]), bf16),
        compiler_params=pltpu.CompilerParams(vmem_limit_bytes=8 * MIB),
        name="spare_facts",
    )(lengths, loss_mask, target)


def stage_kernel(hbm_weight, hbm_cap, weight_ref, cap_ref, sems):
    copies = [
        pltpu.make_async_copy(hbm_weight, weight_ref, sems.at[0]),
        pltpu.make_async_copy(hbm_cap, cap_ref, sems.at[1]),
    ]
    for copy in copies:
        copy.start()
    for copy in copies:
        copy.wait()


def stage(weight, captured):
    return pl.pallas_call(
        stage_kernel,
        in_specs=[FAR, FAR],
        out_specs=[VECTORS] * 2,
        out_shape=(
            jax.ShapeDtypeStruct(weight.shape, bf16),
            jax.ShapeDtypeStruct(captured.shape, bf16),
        ),
        scratch_shapes=[pltpu.SemaphoreType.DMA((2,))],
        compiler_params=pltpu.CompilerParams(vmem_limit_bytes=8 * MIB),
        name="stage",
    )(weight, captured)


def split_by_core(block, first, mine_ref, other_ref, extra=None):
    for j in range(8):
        upper = block[0:PIECE, j * 128 : (j + 1) * 128]
        lower = block[PIECE:ROWS, j * 128 : (j + 1) * 128]
        mine = jnp.where(first, upper, lower)
        other = jnp.where(first, lower, upper)
        if extra is not None:
            mine = jnp.concatenate([mine, extra], axis=0)
            other = jnp.concatenate([other, jnp.zeros_like(extra)], axis=0)
        mine_ref[j] = mine.astype(bf16)
        other_ref[j] = other.astype(bf16)


def unite_kernel(*refs):
    blocks, length_refs = refs[:GROUPS], refs[GROUPS : GROUPS + 3]
    weight_ref, near_rows_ref, far_rows_ref, mine_ref, other_ref, slot_ref = refs[GROUPS + 3 :]
    lengths = [jnp.broadcast_to(ref[0:1, 0:1], (1, 512)) for ref in length_refs]
    lengths = {0: lengths[0], 3: lengths[1], 1: lengths[2], 2: GROUPS * ROWS - sum(lengths)}
    first = lax.axis_index("c") == 0
    groups = [group_at(*place) for place in PLACES]
    lane = lax.broadcasted_iota(jnp.int32, (1, 512), 1).astype(f32)
    have = [
        jnp.clip(
            lengths[dx]
            - lax.rem(lax.axis_index("yh") + dy, 2).astype(f32) * HALF,
            0.0,
            float(HALF),
        )
        for dx, dy in PLACES
    ]
    more = [jnp.maximum(h - ROWS, 0.0) for h in have]
    less = [jnp.maximum(ROWS - h, 0.0) for h in have]

    def before(amounts, k):
        total = jnp.zeros((1, 512), f32)
        for m in range(GROUPS):
            if m != k:
                total = total + amounts[m] * (groups[m] < groups[k]).astype(f32)
        return total

    order = jnp.full((1, 512), -1.0, f32)
    for k in range(GROUPS):
        place = lane - SPARE * k
        mine = (place >= 0) & (place < SPARE)
        order = jnp.where(mine & (place < have[k] - ROWS), before(more, k) + place, order)
    slot = jnp.full((1, 512), -1.0, f32)
    for k in range(GROUPS):
        offset = order - before(less, k)
        mine = (order >= 0) & (offset >= 0) & (offset < ROWS - have[k])
        slot = jnp.where(mine, ROWS * k + have[k] + offset, slot)
    slot_ref[...] = jnp.broadcast_to(slot, (8, 512))
    for half in range(2):
        row = lax.broadcasted_iota(jnp.int32, (4 * ROWS, 384), 0) + half * 4 * ROWS
        pick = (row.astype(f32) == slot[:, :384]).astype(bf16)
        total = None
        for s in range(3):
            pool = jnp.concatenate([block[s, ROWS:HALF, :] for block in blocks], axis=0)
            moved = jnp.dot(pick, pool, preferred_element_type=f32)
            kept = []
            for k in range(4 * half, 4 * half + 4):
                own = blocks[k][s, 0:ROWS, :].astype(f32)
                within = lax.broadcasted_iota(jnp.int32, (ROWS, 512), 0).astype(f32) < have[k]
                base = (k - 4 * half) * ROWS
                kept.append(jnp.where(within, own, moved[base : base + ROWS]))
            upper = jnp.concatenate([rows[0:PIECE] for rows in kept], axis=0)
            lower = jnp.concatenate([rows[PIECE:ROWS] for rows in kept], axis=0)
            part = pl.ds(half * 4 * PIECE, 4 * PIECE)
            near_rows_ref[s, part, :] = jnp.where(first, upper, lower).astype(bf16)
            far_rows_ref[s, part, :] = jnp.where(first, lower, upper).astype(bf16)
            rows = jnp.concatenate(kept, axis=0).astype(bf16)
            term = jnp.dot(rows, weight_ref[s], preferred_element_type=f32)
            total = term if total is None else total + term
        for k in range(4):
            group = groups[4 * half + k]
            split_by_core(
                total[k * ROWS : (k + 1) * ROWS], first, mine_ref.at[group], other_ref.at[group]
            )


def unite(blocks, lengths, weight):
    return pl.pallas_call(
        unite_kernel,
        in_specs=[VECTORS] * (GROUPS + 4),
        out_specs=[VECTORS] * 5,
        out_shape=(
            jax.ShapeDtypeStruct((3, GROUPS * PIECE, 512), bf16),
            jax.ShapeDtypeStruct((3, GROUPS * PIECE, 512), bf16),
            jax.ShapeDtypeStruct((GROUPS, 8, PIECE, 128), bf16),
            jax.ShapeDtypeStruct((GROUPS, 8, PIECE, 128), bf16),
            jax.ShapeDtypeStruct((8, 512), f32),
        ),
        compiler_params=pltpu.CompilerParams(vmem_limit_bytes=24 * MIB),
        name="unite",
    )(*blocks, *lengths, weight)


def head_kernel(
    own_ref, other_ref, gain_ref, head_ref,
    logit_ref, scale_ref, united_ref, held, wide, normed, sems,
):
    width = wide.shape[1]
    tile = head_ref.shape[0] // 8
    loads = [
        pltpu.make_async_copy(
            head_ref.at[pl.ds(i * tile, tile)], held.at[pl.ds(i * tile, tile)], sems.at[i]
        )
        for i in range(8)
    ]
    for copy in loads[:3]:
        copy.start()

    first = lax.axis_index("c") == 0
    wide[ROWS:HALF, :] = jnp.zeros((HALF - ROWS, width), f32)
    for g in range(GROUPS):
        for j in range(8):
            column = (g * 8 + j) * 128
            a = own_ref[j, g].astype(f32)
            b = other_ref[j, g].astype(f32)
            wide[0:PIECE, column : column + 128] = jnp.where(first, a, b)
            wide[PIECE:ROWS, column : column + 128] = jnp.where(first, b, a)
    square = jnp.zeros((HALF, 1), f32)
    for g in range(GROUPS):
        values = wide[:, g * 1024 : (g + 1) * 1024]
        square = square + jnp.sum(values * values, axis=1, keepdims=True)
    scale = lax.rsqrt(square / width + NORM_EPS)
    for g in range(GROUPS):
        part = slice(g * 1024, (g + 1) * 1024)
        values = wide[:, part]
        united_ref[:, part] = values[0:ROWS].astype(bf16)
        normed[part, :] = jnp.transpose(values * scale * gain_ref[:, part]).astype(bf16)

    scale_ref[...] = jnp.transpose(jnp.broadcast_to(scale, (HALF, HALF)))[0:8]
    for i in range(8):
        loads[i].wait()
        if i + 3 < 8:
            loads[i + 3].start()
        part = slice(i * tile, (i + 1) * tile)
        logit_ref[part, :] = jnp.dot(held[part, :], normed[...], preferred_element_type=f32)


def head_forward(own, other, gain, head):
    vocab, width = head.shape
    return pl.pallas_call(
        head_kernel,
        in_specs=[VECTORS] * 3 + [FAR],
        out_specs=[VECTORS] * 4,
        out_shape=(
            jax.ShapeDtypeStruct((vocab, HALF), f32),
            jax.ShapeDtypeStruct((8, HALF), f32),
            jax.ShapeDtypeStruct((ROWS, width), bf16),
            jax.ShapeDtypeStruct((vocab, width), bf16),
        ),
        scratch_shapes=[
            pltpu.VMEM((HALF, width), f32),
            pltpu.VMEM((width, HALF), bf16),
            pltpu.SemaphoreType.DMA((8,)),
        ],
        compiler_params=pltpu.CompilerParams(vmem_limit_bytes=24 * MIB),
        cost_estimate=pl.CostEstimate(
            flops=4 * HALF * vocab * width, bytes_accessed=2 * vocab * width, transcendentals=0
        ),
        name="head_forward",
    )(own, other, gain, head)


def stat_kernel(
    length_ref, logit_ref, scale_ref, target_ref, mask_ref, slot_ref, *refs
):
    spares = refs[:4]
    chosen_ref, stat_ref, side_ref, pool, pool_sems = refs[4:]
    moves = [
        pltpu.make_async_copy(spares[-dx % 4].at[dy], pool.at[k], pool_sems.at[k])
        for k, (dx, dy) in enumerate(PLACES)
    ]
    for copy in moves:
        copy.start()
    for copy in moves:
        copy.wait()
    have = have_here(length_ref[0])
    row = lax.broadcasted_iota(jnp.int32, (HALF, 384), 0)
    pick = (row.astype(f32) == slot_ref[0:1, 0:384]).astype(bf16)
    spare = pool[:, 0:SPARE, :].reshape(384, pool.shape[2])
    moved = jnp.dot(pick, spare, preferred_element_type=f32)
    kept = lax.broadcasted_iota(jnp.int32, moved.shape, 0) < have
    chosen = jnp.transpose(jnp.where(kept, target_ref[...].astype(f32), moved))
    chosen_ref[...] = chosen
    column = lax.broadcasted_iota(jnp.int32, (1, 384), 1)
    mask_pool = seq_pool = jnp.zeros((1, 384), f32)
    counts = []
    for k, place in enumerate(PLACES):
        mine = (column >= SPARE * k) & (column < SPARE * (k + 1))
        facts = pool[k, SPARE : SPARE + 16, :].astype(f32)
        mask_pool = jnp.where(mine, facts[0:1, 0:384], mask_pool)
        seq_pool = jnp.where(mine, (group_at(*place) // 2).astype(f32), seq_pool)
        counts.append(facts[1:2, 0:HALF])
    none = jnp.zeros((6, 384), f32)
    traits = lax.dot_general(
        jnp.concatenate([mask_pool, seq_pool, none], axis=0).astype(bf16), pick, (((1,), (1,)), ((), ())), preferred_element_type=f32
    )
    lane = lax.broadcasted_iota(jnp.int32, (1, HALF), 1)
    masked = (mask_ref[...] == 1).astype(f32)
    valid = jnp.where(lane < have, masked, traits[0:1])
    valid = jnp.where(lane < ROWS, valid, 0.0)
    sequence = jnp.where(lane < have, lax.axis_index("x").astype(f32), traits[1:2])
    nothing = jnp.zeros((1, HALF), f32)
    side_ref[...] = jnp.concatenate(
        [scale_ref[0:1], valid, sequence, sum(counts), counts[0] + counts[1]] + [nothing] * 3, axis=0
    )

    top_t = jnp.max(chosen, axis=0, keepdims=True)
    pow_t = jnp.exp(chosen - top_t)
    sum_t = jnp.sum(pow_t, axis=0, keepdims=True)
    dot_t = jnp.sum(pow_t * chosen, axis=0, keepdims=True)
    logits = logit_ref[...]
    top_d = jnp.max(logits, axis=0, keepdims=True)
    pow_d = jnp.exp(logits - top_d)
    stat_ref[...] = jnp.concatenate(
        [
            top_t,
            sum_t,
            dot_t,
            jnp.sum(pow_t * logits, axis=0, keepdims=True),
            top_d,
            jnp.sum(pow_d, axis=0, keepdims=True),
            jnp.sum(pow_d * logits, axis=0, keepdims=True),
            nothing,
        ],
        axis=0,
    )


def row_stats(lengths, logits, scales, target, loss_mask, slots, spares):
    vocab = logits.shape[0]
    return pl.pallas_call(
        stat_kernel,
        in_specs=[SCALARS] + [VECTORS] * 5 + [FAR] * 4,
        out_specs=[VECTORS] * 3,
        out_shape=(
            jax.ShapeDtypeStruct((vocab, HALF), f32),
            jax.ShapeDtypeStruct((8, HALF), f32),
            jax.ShapeDtypeStruct((8, HALF), f32),
        ),
        scratch_shapes=[
            pltpu.VMEM((GROUPS, SPARE + 16, vocab), bf16),
            pltpu.SemaphoreType.DMA((GROUPS,)),
        ],
        compiler_params=pltpu.CompilerParams(vmem_limit_bytes=16 * MIB),
        name="row_stats",
    )(lengths, logits, scales, target, loss_mask, slots, *spares)


def back_kernel(
    every_ref, logit_ref, chosen_ref, side_ref, gain_ref, united_ref, head_ref,
    mine_ref, other_ref,
):
    width = gain_ref.shape[1]
    every = every_ref[...]
    max_t = jnp.max(every[:, 0:1], axis=0)
    scale_t = jnp.exp(every[:, 0:1] - max_t[None])
    sum_t = jnp.sum(every[:, 1:2] * scale_t, axis=0)
    mean_tt = jnp.sum(every[:, 2:3] * scale_t, axis=0) / sum_t
    mean_tl = jnp.sum(every[:, 3:4] * scale_t, axis=0) / sum_t
    max_d = jnp.max(every[:, 4:5], axis=0)
    scale_d = jnp.exp(every[:, 4:5] - max_d[None])
    sum_d = jnp.sum(every[:, 5:6] * scale_d, axis=0)
    mean_dl = jnp.sum(every[:, 6:7] * scale_d, axis=0) / sum_d
    log_t = max_t + jnp.log(sum_t)
    log_d = max_d + jnp.log(sum_d)
    row_scale, valid, sequence = side_ref[0:1], side_ref[1:2], side_ref[2:3]
    kl = (mean_tt - mean_tl - log_t + log_d) * valid
    row = lax.broadcasted_iota(jnp.int32, (8, HALF), 0)
    sums = jnp.sum(jnp.where(row.astype(f32) == sequence, kl, 0.0), axis=1, keepdims=True)
    sums = jnp.broadcast_to(sums, (8, HALF))
    high = sums.astype(bf16).astype(f32)
    middle = (sums - high).astype(bf16).astype(f32)
    column = lax.broadcasted_iota(jnp.int32, (8, HALF), 1)
    third = jnp.where(column < 96, sums - high - middle, 0.0)
    sums = jnp.where(column < 32, high, jnp.where(column < 64, middle, third))

    weight = valid * row_scale
    grad = weight * (jnp.exp(logit_ref[...] - log_d) - jnp.exp(chosen_ref[...] - log_t))
    grad = jnp.transpose(grad)[0:ROWS].astype(bf16)
    lane = lax.broadcasted_iota(jnp.int32, (1, HALF), 1)
    share = ROWS // 16
    index = lax.axis_index(("z", "yl", "c"))
    mine = (lane >= index * share) & (lane < (index + 1) * share)
    cubic = jnp.where(mine, weight * row_scale * (mean_dl - mean_tl) / width, 0.0)
    cubic = jnp.transpose(jnp.broadcast_to(cubic, (HALF, HALF)))[0:ROWS, 0:1]
    for g in range(GROUPS):
        part = slice(g * 1024, (g + 1) * 1024)
        block = jnp.dot(grad, head_ref[:, part], preferred_element_type=f32)
        block = block * gain_ref[:, part] - cubic * united_ref[:, part].astype(f32)
        split_by_core(
            block, lax.axis_index("c") == 0, mine_ref.at[g], other_ref.at[g], sums
        )


def head_backward(every, logits, chosen, side, gain, united, head):
    return pl.pallas_call(
        back_kernel,
        in_specs=[VECTORS] * 7,
        out_specs=[VECTORS] * 2,
        out_shape=(
            jax.ShapeDtypeStruct((GROUPS, 8, PIECE + 8, 128), bf16),
            jax.ShapeDtypeStruct((GROUPS, 8, PIECE + 8, 128), bf16),
        ),
        compiler_params=pltpu.CompilerParams(vmem_limit_bytes=24 * MIB),
        name="head_backward",
    )(every, logits, chosen, side, gain, united, head)


def assemble(grad_ref, wide, grads):
    for k, place in enumerate(PLACES):
        group = group_at(*place)
        for j in range(8):
            wide[k * PIECE : (k + 1) * PIECE, j * 128 : (j + 1) * 128] = grad_ref[
                j, group
            ].astype(f32)
    grads[...] = wide[...].astype(bf16)


def near_kernel(grad_ref, rows_ref, out_ref, wide, grads):
    assemble(grad_ref, wide, grads)
    for s in range(3):
        out_ref[s] = lax.dot_general(
            rows_ref[s], grads[...], (((0,), (0,)), ((), ())), preferred_element_type=f32
        )


def far_kernel(side_ref, grad_ref, rows_ref, near_ref, out_ref, wide, grads, done, sems):
    assemble(grad_ref, wide, grads)
    factor = (2 * HALF) / jnp.maximum(side_ref[3:4, 0:1], 1.0)
    copies = []
    for s in range(3):
        for i in range(2):
            part = slice(i * 256, (i + 1) * 256)
            done[s, part, :] = factor * (
                near_ref[s, part, :]
                + lax.dot_general(
                    rows_ref[s, :, part],
                    grads[...],
                    (((0,), (0,)), ((), ())),
                    preferred_element_type=f32,
                )
            )
            copies.append(
                pltpu.make_async_copy(
                    done.at[s, pl.ds(i * 256, 256)],
                    out_ref.at[s, pl.ds(i * 256, 256)],
                    sems.at[2 * s + i],
                )
            )
            copies[-1].start()
    for copy in copies:
        copy.wait()


def near_gradient(own, rows):
    total = GROUPS * PIECE
    return pl.pallas_call(
        near_kernel,
        in_specs=[VECTORS] * 2,
        out_specs=VECTORS,
        out_shape=jax.ShapeDtypeStruct((3, 512, 1024), f32),
        scratch_shapes=[pltpu.VMEM((total, 1024), f32), pltpu.VMEM((total, 1024), bf16)],
        compiler_params=pltpu.CompilerParams(vmem_limit_bytes=16 * MIB),
        cost_estimate=pl.CostEstimate(
            flops=6 * total * 512 * 1024, bytes_accessed=6 * MIB, transcendentals=0
        ),
        name="near_gradient",
    )(own, rows)


def weight_gradient(side, other, rows, near):
    total = GROUPS * PIECE
    return pl.pallas_call(
        far_kernel,
        in_specs=[VECTORS] * 4,
        out_specs=FAR,
        out_shape=jax.ShapeDtypeStruct((3, 512, 1024), f32),
        scratch_shapes=[
            pltpu.VMEM((total, 1024), f32),
            pltpu.VMEM((total, 1024), bf16),
            pltpu.VMEM((3, 512, 1024), f32),
            pltpu.SemaphoreType.DMA((6,)),
        ],
        compiler_params=pltpu.CompilerParams(vmem_limit_bytes=24 * MIB),
        name="weight_gradient",
    )(side, other, rows, near)


def sum_kernel(piece_ref, out_ref, extra_ref):
    extra = jnp.zeros((8, 128), f32)
    for g in range(GROUPS):
        total = jnp.zeros((PIECE, 128), f32)
        for j in range(8):
            total = total + piece_ref[g * 8 + j, 0:PIECE, :].astype(f32)
        for k in range(8):
            out_ref[k, g] = total.astype(bf16)
        if piece_ref.shape[1] > PIECE:
            extra = extra + piece_ref[g * 8].astype(f32)[PIECE : PIECE + 8]
    extra_ref[...] = extra


def gather_sum(mine, other):
    pair = (mine.astype(f32) + swap(other, "c", 1, 2).astype(f32)).astype(bf16)
    received = lax.all_to_all(pair.reshape((64,) + pair.shape[2:]), CHIPS, 0, 0, tiled=True)
    copies, extra = pl.pallas_call(
        sum_kernel,
        in_specs=[VECTORS],
        out_specs=[VECTORS] * 2,
        out_shape=(
            jax.ShapeDtypeStruct((8, GROUPS, PIECE, 128), bf16),
            jax.ShapeDtypeStruct((8, 128), f32),
        ),
        compiler_params=pltpu.CompilerParams(vmem_limit_bytes=8 * MIB),
        name="sum_pieces",
    )(received)
    return copies, extra


def route(value, dx, dy):
    pairs = [(p * 2 + q, (p + dx) % 4 * 2 + (q ^ dy)) for p in range(4) for q in range(2)]
    return lax.ppermute(value, GROUP, pairs)


def local(captured, target_logits, unite_weight, norm_gain, head_weight, lengths, loss_mask):
    width = norm_gain.shape[0]
    own = captured.reshape(3, HALF, 512)
    target = target_logits.reshape(HALF, -1)
    far = route(own, 2, 0)
    over = route(own, 0, 1)
    right = route(own, 3, 0)
    left = route(own, 1, 0)
    far, near_target, later = lax.optimization_barrier((far, target, lengths))
    over_far = route(far, 0, 1)
    over_right = route(over, 3, 0)
    over_left = route(over, 1, 0)
    spare = spare_facts(lengths, loss_mask, near_target)
    pair = jnp.stack([spare, route(spare, 0, 1)])
    wide_length = jnp.broadcast_to(later.astype(f32), (8, HALF))
    all_lengths = [wide_length, route(wide_length, 1, 0), route(wide_length, 3, 0)]
    left, right, weight, all_lengths[1] = lax.optimization_barrier(
        (left, right, unite_weight, all_lengths[1])
    )
    weight, near = stage(weight, own)
    over_far, pair = lax.optimization_barrier((over_far, pair))
    blocks = [near, over, left, right, far, over_left, over_right, over_far]
    near_rows, far_rows, mine, other, slots = unite(blocks, all_lengths, weight)

    copies, _ = gather_sum(mine, other)
    copies, pair = lax.optimization_barrier((copies, pair))
    spares = [pair] + [route(pair, dx, 0) for dx in range(1, 4)]
    own_united = lax.all_to_all(copies, RING, 0, 0, tiled=True)
    own_united, spares[1], spares[3] = lax.optimization_barrier(
        (own_united, spares[1], spares[3])
    )
    other_united = swap(own_united, "c", 1, 2)
    gain = norm_gain.reshape(1, width)
    logits, scales, united, held = head_forward(own_united, other_united, gain, head_weight)
    chosen, stats, side = row_stats(
        lengths, logits, scales, target, loss_mask, slots, spares
    )
    every = spread(stats, ("z", "yl", "c"), 16)
    mine, other = head_backward(every, logits, chosen, side, gain, united, held)
    copies, sums = gather_sum(mine, other)
    own_grad = lax.all_to_all(copies, RING, 0, 0, tiled=True)
    seq_sum = jnp.sum(
        jnp.where(lax.iota(jnp.int32, GROUPS)[:, None] == lax.axis_index("x"), sums, 0.0)
    )
    seq_kl = (seq_sum / 32.0 / jnp.maximum(side[4, 0], 1.0)).reshape(1)
    own_grad, seq_kl = lax.optimization_barrier((own_grad, seq_kl))
    other_grad = swap(own_grad, "c", 1, 2)
    near_part = near_gradient(own_grad, near_rows)
    unite_grad = weight_gradient(side, other_grad, far_rows, near_part)
    return (seq_kl, unite_grad)


def solution(mesh):
    fine = Mesh(mesh.devices.reshape(4, 2, 4, 2, 2), ALL)
    tensor = ("z", "yl", "c")
    placed = (
        P(None, "x", "yh", tensor),
        P("x", "yh", tensor),
        P(None, tensor, GROUP),
        P(),
        P(tensor, None),
        P("x"),
        P("x", "yh"),
    )
    return jax.shard_map(
        local,
        mesh=fine,
        in_specs=placed,
        out_specs=(P("x"), P(None, tensor, GROUP)),
        check_vma=False,
    )
```
